32 devices in a mesh: grp: 2 (over y), occ: 4 (over x, core), aux: 4 (over z).
Axes of the slice: x: 2, y: 2, z: 4, core: 2. Of those that a mesh axis runs over, the one named last changes fastest.
Arguments:
- bmat: bfloat16 [8, 6144, 1536], P(('grp', 'occ'), 'aux'), parts along dimension 0, may hold values from -0.625 to 0.625
- eps_occ: float32 [8], P('grp'), parts along dimension 0, may hold values from -1.5 to -0.5
- eps_vir: float32 [3072], P('grp'), parts along dimension 0, may hold values from 0.2 to 3
- occ_label: int32 [8], P('grp'), parts along dimension 0, may hold values from 0 to 3, each once
Outputs:
- gamma: bfloat16 [8, 6144, 1536], P(('grp', 'occ'), 'aux'), parts along dimension 0
- density: float32 [3072, 1536], P(('grp', 'aux'), 'occ'), parts along dimension 0
The draws below stay inside these ranges and needn't reach their ends.
There are 2 independent parts, one for each index of `grp`. The reference program is written for one: setup_inputs(seed, part) draws one part's arguments, and reference() takes and returns one part's arrays. A program takes and returns all parts, laid end to end along the dimension named above; each array names one. Nothing has to cross between parts.
Inputs may be any that keep to these rules, and one draw needn't show every extreme that they name: `occ_label`: a permutation: each label appears once.
All inputs are finite; a program needn't handle non-finite values.
Results may differ from the reference program's by a relative error of at most 0.008.
Values may be sent and summed in bfloat16 or wider, within the bound.
No kernel may reach another device: no remote copies, remote signals or barrier semaphores. Data moves between devices by JAX's collectives and lax.ppermute only.
A program may use at most 128 MiB of HBM per device.

```python
import jax
import jax.numpy as jnp
from jax import lax

NVIR = 1536
NAUX = 6144
OCC_WIN = 4
N_AUX = 4


def levels(own_key, dims, cuts, least, top_value):
    def one(position, shards_of):
        heights = jax.random.uniform(jax.random.fold_in(jax.random.fold_in(own_key, 6), position), (shards_of,), jnp.float32, least / len(cuts), top_value / len(cuts))
        return jnp.repeat(jnp.exp(heights), dims[position] // shards_of).reshape((-1,) + (1,) * (len(dims) - position - 1))

    level = one(*cuts[0])
    for cut in cuts[1:]:
        level = level * one(*cut)
    return level


def noise(key, extent, spread, bound, cuts=(), dtype=jnp.bfloat16):
    factor_of = levels(key, extent, cuts, -0.22, 0.18) if cuts else 1.0
    result = jax.random.normal(key, extent, jnp.float32) * spread * factor_of
    return jnp.minimum(jnp.maximum(result, -bound), bound).astype(dtype)


def setup_inputs(seed: int = 0, part: int = 0) -> dict:
    arg_keys = jax.random.split(jax.random.key(seed), 5)
    part_keys = jax.random.split(jax.random.fold_in(arg_keys[4], part), 5)
    bmat = noise(part_keys[0], (OCC_WIN, NAUX, NVIR), (NAUX ** -0.25), 0.625, ((0, 4), (1, 4)))
    eps_occ = jnp.clip(jax.random.uniform(part_keys[1], (OCC_WIN,), jnp.float32, -1.5, -0.5), -1.5, -0.5)
    eps_vir = jnp.clip(jax.random.uniform(part_keys[2], (NVIR,), jnp.float32, 0.2, 3.0), 0.2, 3.0)
    occ_label = jax.random.permutation(part_keys[3], OCC_WIN).astype(jnp.int32)
    return dict(bmat=bmat, eps_occ=eps_occ, eps_vir=eps_vir, occ_label=occ_label)


def reference(bmat, eps_occ, eps_vir, occ_label):
    count = bmat.shape[0]
    energy = jnp.take(eps_occ, occ_label)
    slabs = bmat.reshape(count, N_AUX, NAUX // N_AUX, NVIR)
    contract = (((1,), (1,)), ((), ()))
    density = jnp.zeros((NVIR, NVIR), jnp.float32)
    owned = []
    returned = []
    for row in range(count):
        prev = (row - 1) % count
        mine = slabs[row].astype(jnp.float32)
        other = slabs[prev].astype(jnp.float32)
        partial_value = jnp.einsum("kqa,kqb->kab", mine, other, precision=lax.Precision.HIGHEST)
        partial_value = lax.optimization_barrier(partial_value.astype(jnp.bfloat16))
        summed = jnp.sum(partial_value.astype(jnp.float32), axis=0)
        denom = eps_vir[:, None] + eps_vir[None, :] - energy[row] - energy[prev]
        amp = (summed / denom).astype(jnp.bfloat16)
        amp_wide = amp.astype(jnp.float32)
        tilde = (2.0 * amp_wide - amp_wide.T).astype(jnp.bfloat16)
        owned.append(lax.dot_general(bmat[prev], tilde, contract, preferred_element_type=jnp.float32))
        returned.append(jnp.dot(bmat[row], tilde, preferred_element_type=jnp.float32).astype(jnp.bfloat16))
        density = density + lax.dot_general(amp, tilde, contract, preferred_element_type=jnp.float32)
    pieces = []
    for row in range(count):
        pieces.append((owned[row] + returned[(row + 1) % count].astype(jnp.float32)).astype(jnp.bfloat16))
    gamma = jnp.stack(pieces, axis=0)
    return gamma, density * (NVIR ** -0.5)
```

```python
import jax
import jax.numpy as jnp
from jax import lax
from jax.sharding import PartitionSpec as P

CHUNKS = 4
F32 = jnp.float32
BF16 = jnp.bfloat16


def contract(left, right, dim_left, dim_right):
    return lax.dot_general(
        left, right, (((dim_left,), (dim_right,)), ((), ())), preferred_element_type=F32
    )


def slab_sum_scale(part, denom, slabs, slab_index):
    if slabs != 4:
        rows, cols = part.shape
        blocks = part.reshape(slabs, rows // slabs, cols)
        blocks = lax.all_to_all(blocks, "aux", split_axis=0, concat_axis=0, tiled=True)
        total = jnp.sum(blocks.astype(F32), axis=0).astype(BF16)
        total = lax.all_gather(total, "aux", axis=0, tiled=True)
        return (total.astype(F32) / denom).astype(BF16)
    inner = (slab_index == 1) | (slab_index == 2)
    inward = lax.ppermute(part, "aux", [(0, 1), (3, 2)])
    half = (part.astype(F32) + inward.astype(F32)).astype(BF16)
    across = lax.ppermute(half, "aux", [(1, 2), (2, 1)])
    amp = ((half.astype(F32) + across.astype(F32)) / denom).astype(BF16)
    outward = lax.ppermute(amp, "aux", [(1, 0), (2, 3)])
    return jnp.where(inner, amp, outward)


def shards(bmat, eps_occ, eps_vir, occ_label):
    count = lax.axis_size("occ")
    slabs = lax.axis_size("aux")
    place = lax.axis_index("occ")
    slab_index = lax.axis_index("aux")
    chips = count // 2
    chip, core = place // 2, place % 2
    first = core == 0
    nvirt = eps_vir.shape[0]
    half = nvirt // 2
    width = half // CHUNKS
    labels = jnp.arange(count, dtype=jnp.int32)
    energy = jnp.sum(
        eps_occ[None, :] * (occ_label[:, None] == labels[None, :]).astype(F32), axis=1
    )
    swap_pairs = [(i, i ^ 1) for i in range(count)]

    def energy_at(row):
        return lax.dynamic_index_in_dim(energy, (row + count) % count, 0, keepdims=False)

    def swapped(value):
        return lax.ppermute(value, "occ", swap_pairs)

    energy_cross = energy_at(2 * chip), energy_at(2 * chip - 1)
    energy_local = energy_at(2 * chip + 1), energy_at(2 * chip)

    mine = bmat[0]
    partner = swapped(mine)
    even = jnp.where(first, mine, partner)
    odd = jnp.where(first, partner, mine)

    def arrived(j):
        start = j * width
        sent = jnp.where(
            first, partner[:, start : start + width], mine[:, half + start : half + start + width]
        )
        return lax.ppermute(sent, "occ", [(i, (i + 2) % count) for i in range(count)])

    incoming = [arrived(j) for j in range(CHUNKS)]

    def scaled(part, j, energies):
        eps_rows = lax.dynamic_slice_in_dim(eps_vir, core * half + j * width, width)
        denom = eps_rows[:, None] + eps_vir[None, :] - energies[0] - energies[1]
        return slab_sum_scale(part, denom, slabs, slab_index)

    def cross(j):
        return scaled(contract(incoming[j], even, 0, 0).astype(BF16), j, energy_cross)

    def local(j):
        cols = lax.dynamic_slice_in_dim(even, core * half + j * width, width, axis=1)
        return scaled(contract(cols, odd, 0, 0).astype(BF16), j, energy_local)

    local_parts = [local(0)]
    cross_parts = [cross(j) for j in range(CHUNKS)]
    local_parts += [local(j) for j in range(1, CHUNKS)]

    def whole(parts):
        mine_rows = jnp.concatenate(parts, axis=0)
        other_rows = swapped(mine_rows)
        return jnp.concatenate(
            [jnp.where(first, mine_rows, other_rows), jnp.where(first, other_rows, mine_rows)], axis=0
        )

    def mixed(amp_t, straight):
        wide = amp_t.astype(F32)
        turned = wide.T
        return jnp.where(straight, 2.0 * wide - turned, 2.0 * turned - wide).astype(BF16)

    def density_part(amp_t):
        rows = nvirt // slabs
        cols = nvirt // count
        amp_rows = lax.dynamic_slice_in_dim(amp_t, slab_index * rows, rows, axis=1)
        pieces = []
        for ahead in range(chips):
            start = (2 * ((chip + ahead) % chips) + core) * cols
            straight = lax.dynamic_slice_in_dim(amp_t, start, cols, axis=1).astype(F32)
            turned = lax.dynamic_slice_in_dim(amp_t, start, cols, axis=0).astype(F32).T
            tilde_t = (2.0 * straight - turned).astype(BF16)
            pieces.append(contract(amp_rows, tilde_t, 0, 0))
        return pieces

    cross_t = whole(cross_parts)
    cross_mix = mixed(cross_t, first)
    received = jnp.concatenate(incoming, axis=1)
    upper = swapped(received)
    left = jnp.where(first, jnp.concatenate([received, upper], axis=1), partner)
    step = nvirt // CHUNKS
    cross_out, returned = [], []
    back_pairs = [(i, (i - 2) % count) for i in range(1, count, 2)]
    for j in range(CHUNKS):
        out = jnp.dot(left, cross_mix[:, j * step : (j + 1) * step], preferred_element_type=F32)
        back = lax.ppermute(out.astype(BF16), "occ", back_pairs)
        cross_out.append(out)
        returned.append(back)
    cross_density = density_part(cross_t)

    local_t = whole(local_parts)
    local_mix = mixed(local_t, ~first)
    local_out = jnp.dot(partner, local_mix, preferred_element_type=F32)
    local_density = density_part(local_t)

    scale = nvirt ** (-0.5)
    pieces = [(a + b) * scale for a, b in zip(cross_density, local_density)]
    density = pieces[0]
    for ahead in range(1, chips):
        pairs = [(i, (i + 2 * ahead) % count) for i in range(count)]
        density = density + lax.ppermute(pieces[ahead].astype(BF16), "occ", pairs).astype(F32)

    gamma = []
    for j in range(CHUNKS):
        term = jnp.where(first, cross_out[j], returned[j].astype(F32))
        gamma.append((local_out[:, j * step : (j + 1) * step] + term).astype(BF16))
    return jnp.concatenate(gamma, axis=1)[None], density


def solution(mesh):
    return jax.shard_map(
        shards,
        mesh=mesh,
        in_specs=(P(("grp", "occ"), "aux", None), P("grp"), P("grp"), P("grp")),
        out_specs=(P(("grp", "occ"), "aux", None), P(("grp", "aux"), "occ")),
        check_vma=False,
    )
```

```python
import functools

import jax
import jax.numpy as jnp
from jax import lax
from jax.experimental import pallas as pl
from jax.experimental.pallas import tpu as pltpu
from jax.sharding import PartitionSpec as P

F32 = jnp.float32
BF16 = jnp.bfloat16
PIECES = 3
LIMIT = 48 * 1024 * 1024


def contract(left, right, dim_left, dim_right):
    return lax.dot_general(
        left, right, (((dim_left,), (dim_right,)), ((), ())), preferred_element_type=F32
    )


class Order:
    def __init__(self, first):
        self.last = first

    def ready(self, *values):
        return lax.optimization_barrier((*values, self.last))[:-1]

    def step(self, work, *values):
        result = work(*self.ready(*values))
        self.last = result
        return result

    def send(self, value, axis, pairs, *others):
        return lax.ppermute(self.ready(value, *others)[0], axis, pairs)


def mix_kernel(half, band, rows, cols, straight_core, place, *refs):
    pieces, (mix, dens, amp_t, amp, sems) = refs[: 2 * PIECES], refs[2 * PIECES :]
    core, slab, chip = place[0], place[1], place[2]
    nvirt = 2 * half
    width = half // PIECES
    step = pl.program_id(0)

    @pl.when(step == 0)
    def _():
        copies = []
        for i, piece in enumerate(pieces):
            side = core if i < PIECES else 1 - core
            start = pl.multiple_of(side * half + (i % PIECES) * width, width)
            copies.append(pltpu.make_async_copy(piece, amp_t.at[pl.ds(start, width), :], sems.at[i]))
        for copy in copies:
            copy.start()
        for copy in copies:
            copy.wait()

    straight = core == straight_core
    here = jnp.where(straight, 2.0, -1.0).astype(F32)
    there = jnp.where(straight, -1.0, 2.0).astype(F32)
    start = pl.multiple_of(step * band, band)
    for j in range(nvirt // band):
        tile = amp_t[pl.ds(start, band), j * band : (j + 1) * band].astype(F32)
        turned = amp_t[j * band : (j + 1) * band, pl.ds(start, band)].astype(F32).T
        amp[pl.ds(start, band), j * band : (j + 1) * band] = turned.astype(BF16)
        mix[:, j * band : (j + 1) * band] = (here * tile + there * turned).astype(BF16)

    @pl.when(step == nvirt // band - 1)
    def _():
        chips = dens.shape[0]
        left = amp[pl.ds(pl.multiple_of(slab * rows, rows), rows), :]
        for ahead in range(chips):
            at = pl.multiple_of((2 * lax.rem(chip + ahead, chips) + core) * cols, cols)
            tilde = 2.0 * amp[pl.ds(at, cols), :].astype(F32) - amp_t[pl.ds(at, cols), :].astype(F32)
            dens[ahead] = contract(left, tilde.astype(BF16), 1, 1)


def mix(place, own, other, straight_core, slabs, count):
    width, nvirt = own[0].shape
    rows, cols, chips = nvirt // slabs, nvirt // count, count // 2
    band = 256
    return pl.pallas_call(
        functools.partial(mix_kernel, nvirt // 2, band, rows, cols, straight_core),
        grid_spec=pltpu.PrefetchScalarGridSpec(
            num_scalar_prefetch=1,
            grid=(nvirt // band,),
            in_specs=[pl.BlockSpec(memory_space=pl.ANY)] * (2 * PIECES),
            out_specs=[
                pl.BlockSpec((band, nvirt), lambda i, p: (i, 0)),
                pl.BlockSpec((chips, rows, cols), lambda i, p: (0, 0, 0)),
            ],
            scratch_shapes=[
                pltpu.VMEM((nvirt, nvirt), BF16),
                pltpu.VMEM((nvirt, nvirt), BF16),
                pltpu.SemaphoreType.DMA((2 * PIECES,)),
            ],
        ),
        out_shape=[
            jax.ShapeDtypeStruct((nvirt, nvirt), BF16),
            jax.ShapeDtypeStruct((chips, rows, cols), F32),
        ],
        compiler_params=pltpu.CompilerParams(vmem_limit_bytes=LIMIT),
        cost_estimate=pl.CostEstimate(
            flops=2 * rows * cols * chips * nvirt, bytes_accessed=4 * nvirt * nvirt, transcendentals=0
        ),
        name="mix",
    )(place, *own, *other)


def cross_kernel(place, *refs):
    pieces, (partner, weight, out) = refs[: 2 * PIECES], refs[2 * PIECES :]
    width = pieces[0].shape[1]

    @pl.when(place[0] == 0)
    def _():
        total = contract(pieces[0][...], weight[:width, :], 1, 0)
        for i in range(1, 2 * PIECES):
            total += contract(pieces[i][...], weight[i * width : (i + 1) * width, :], 1, 0)
        out[...] = total.astype(BF16)

    @pl.when(place[0] != 0)
    def _():
        out[...] = contract(partner[...], weight[...], 1, 0).astype(BF16)


def cross_columns(place, pieces, partner, weight, j, step):
    rows, nvirt = partner.shape
    width = pieces[0].shape[1]
    block = 256 if rows % 256 == 0 else 128
    return pl.pallas_call(
        cross_kernel,
        grid_spec=pltpu.PrefetchScalarGridSpec(
            num_scalar_prefetch=1,
            grid=(rows // block,),
            in_specs=[pl.BlockSpec((block, width), lambda i, p: (jnp.where(p[0] == 0, i, 0), 0))]
            * (2 * PIECES)
            + [
                pl.BlockSpec((block, nvirt), lambda i, p: (jnp.where(p[0] == 0, 0, i), 0)),
                pl.BlockSpec((nvirt, step), lambda i, p: (0, j)),
            ],
            out_specs=pl.BlockSpec((block, step), lambda i, p: (i, 0)),
        ),
        out_shape=jax.ShapeDtypeStruct((rows, step), BF16),
        compiler_params=pltpu.CompilerParams(vmem_limit_bytes=LIMIT),
        cost_estimate=pl.CostEstimate(
            flops=2 * rows * nvirt * step, bytes_accessed=2 * rows * (nvirt + step), transcendentals=0
        ),
        name="cross_term",
    )(place, *pieces, partner, weight)


def final_kernel(place, partner, weight, kept, arrived, *refs):
    out = refs[-1]
    total = contract(partner[...], weight[...], 1, 0)

    @pl.when(place[0] == 0)
    def _():
        out[0] = (total.astype(BF16).astype(F32) + kept[...].astype(F32)).astype(BF16)

    @pl.when(place[0] != 0)
    def _():
        out[0] = (total + arrived[...].astype(F32)).astype(BF16)


def final_columns(place, partner, weight, kept, arrived, j, step, gamma):
    rows, nvirt = partner.shape
    block = 256 if rows % 256 == 0 else 128
    before = [] if gamma is None else [gamma]
    return pl.pallas_call(
        final_kernel,
        grid_spec=pltpu.PrefetchScalarGridSpec(
            num_scalar_prefetch=1,
            grid=(rows // block,),
            in_specs=[
                pl.BlockSpec((block, nvirt), lambda i, p: (i, 0)),
                pl.BlockSpec((nvirt, step), lambda i, p: (0, j)),
                pl.BlockSpec((block, step), lambda i, p: (jnp.where(p[0] == 0, i, 0), 0)),
                pl.BlockSpec((block, step), lambda i, p: (jnp.where(p[0] == 0, 0, i), 0)),
            ]
            + [pl.BlockSpec(memory_space=pl.ANY)] * len(before),
            out_specs=pl.BlockSpec((1, block, step), lambda i, p: (0, i, j)),
        ),
        out_shape=jax.ShapeDtypeStruct((1, rows, nvirt), BF16),
        input_output_aliases={5: 0} if before else {},
        compiler_params=pltpu.CompilerParams(vmem_limit_bytes=LIMIT),
        cost_estimate=pl.CostEstimate(
            flops=2 * rows * nvirt * step, bytes_accessed=2 * rows * (nvirt + step), transcendentals=0
        ),
        name="local_term",
    )(place, partner, weight, kept, arrived, *before)


def shards(bmat, eps_occ, eps_vir, occ_label):
    count = lax.axis_size("occ")
    slabs = lax.axis_size("aux")
    place = lax.axis_index("occ")
    slab_index = lax.axis_index("aux")
    chips = count // 2
    chip, core = place // 2, place % 2
    first = core == 0
    where = jnp.stack([core, slab_index, chip]).astype(jnp.int32)
    nvirt = eps_vir.shape[0]
    half = nvirt // 2
    width = half // PIECES
    labels = jnp.arange(count, dtype=jnp.int32)
    energy = jnp.sum(
        eps_occ[None, :] * (occ_label[:, None] == labels[None, :]).astype(F32), axis=1
    )
    swap_pairs = [(i, i ^ 1) for i in range(count)]
    next_pairs = [(i, (i + 2) % count) for i in range(count)]
    down_pairs = [(i, i - 1) for i in range(1, count, 2)]
    back_pairs = [(i, (i - 2) % count) for i in range(1, count, 2)]
    inner = (slab_index == 1) | (slab_index == 2)

    def energy_at(row):
        return lax.dynamic_index_in_dim(energy, (row + count) % count, 0, keepdims=False)

    energies = {
        "cross": (energy_at(2 * chip), energy_at(2 * chip - 1)),
        "local": (energy_at(2 * chip + 1), energy_at(2 * chip)),
    }

    mine = bmat[0]
    partner = lax.ppermute(mine, "occ", swap_pairs)
    order = Order(partner)
    incoming, upper = {}, {}

    def ship(j, *others):
        sent = order.step(
            lambda p, m: jnp.where(
                first,
                p[:, j * width : (j + 1) * width],
                m[:, half + j * width : half + (j + 1) * width],
            ),
            partner,
            mine,
        )
        incoming[j] = order.send(sent, "occ", next_pairs, *others)

    ship(0)
    ship(1)
    even = order.step(lambda m, p: jnp.where(first, m, p), mine, partner)
    odd = order.step(lambda m, p: jnp.where(first, p, m), mine, partner)

    def product(kind, j):
        if kind == "cross":
            part = order.step(lambda a, b: contract(a, b, 0, 0).astype(BF16), incoming[j], even)
            if j + 2 < PIECES:
                ship(j + 2)
            upper[j] = order.send(incoming[j], "occ", down_pairs)
            return part
        return order.step(
            lambda a, b: contract(
                lax.dynamic_slice_in_dim(a, core * half + j * width, width, axis=1), b, 0, 0
            ).astype(BF16),
            even,
            odd,
        )

    def scaled(kind, j, mine_sum, other_sum):
        eps_rows = lax.dynamic_slice_in_dim(eps_vir, core * half + j * width, width)
        denom = eps_rows[:, None] + eps_vir[None, :] - energies[kind][0] - energies[kind][1]
        return ((mine_sum.astype(F32) + other_sum.astype(F32)) / denom).astype(BF16)

    own, other = {"cross": [], "local": []}, {"cross": [], "local": []}
    jobs = [("local",0),("cross",0),("cross",1),("cross",2),("local",1),("local",2)]
    n = len(jobs)
    part, inward, summed, across, amp, outward = ({} for _ in range(6))

    def feed(s):
        part[s] = product(*jobs[s])
        inward[s] = order.send(part[s], "aux", [(0, 1), (3, 2)])

    results = {}

    def finish_cross():
        weight, dens = order.step(
            lambda *v: mix(where, v[:PIECES], v[PIECES:], 0, slabs, count), *own["cross"], *other["cross"]
        )
        results["cross_density"] = dens
        kept, arrived = [], []
        pieces = [incoming[j] for j in range(PIECES)] + [upper[j] for j in range(PIECES)]
        step = nvirt // PIECES
        for j in range(PIECES):
            kept.append(
                order.step(lambda w, p, *v: cross_columns(where, v, p, w, j, step), weight, partner, *pieces)
            )
            arrived.append(order.send(kept[j], "occ", back_pairs))
        results["kept"], results["arrived"] = kept, arrived

    done = None
    for s in range(-1, n + 2):
        if s + 1 < n:
            feed(s + 1)
        if done is not None:
            order.last = (order.last, done)
        if 0 <= s < n:
            summed[s] = order.step(
                lambda a, b: (a.astype(F32) + b.astype(F32)).astype(BF16), part[s], inward[s]
            )
        t = s - 1
        if 0 <= t < n:
            amp[t] = order.step(lambda a, b: scaled(*jobs[t], a, b), summed[t], across[t])
        if 0 <= s < n:
            across[s] = order.send(summed[s], "aux", [(1, 2), (2, 1)])
        t = s - 2
        if 0 <= t < n:
            full = order.step(lambda a, b: jnp.where(inner, a, b), amp[t], outward[t])
            kind = jobs[t][0]
            own[kind].append(full)
            done = order.send(full, "occ", swap_pairs)
            other[kind].append(done)
        t = s - 1
        if 0 <= t < n:
            outward[t] = order.send(amp[t], "aux", [(1, 0), (2, 3)])
        if len(own["cross"]) == PIECES and "kept" not in results:
            finish_cross()

    weight, dens = order.step(
        lambda *v: mix(where, v[:PIECES], v[PIECES:], 1, slabs, count), *own["local"], *other["local"]
    )
    total = order.step(lambda a, b: (a + b) * nvirt ** (-0.5), results["cross_density"], dens)
    density = total[0]
    for ahead in range(1, chips):
        pairs = [(i, (i + 2 * ahead) % count) for i in range(count)]
        density = density + order.send(total[ahead].astype(BF16), "occ", pairs).astype(F32)
    gamma = None
    step = nvirt // PIECES
    for j in range(PIECES):
        gamma = order.step(
            lambda p, w, k, a, *g: final_columns(where, p, w, k, a, j, step, *g),
            partner, weight, results["kept"][j], results["arrived"][j], *([None] if gamma is None else [gamma]),
        )
    return gamma, density


def solution(mesh):
    return jax.shard_map(
        shards,
        mesh=mesh,
        in_specs=(P(("grp", "occ"), "aux", None), P("grp"), P("grp"), P("grp")),
        out_specs=(P(("grp", "occ"), "aux", None), P(("grp", "aux"), "occ")),
        check_vma=False,
    )
```

```python
import functools

import jax
import jax.numpy as jnp
from jax import lax
from jax.experimental import pallas as pl
from jax.experimental.pallas import tpu as pltpu
from jax.sharding import PartitionSpec as P

F32 = jnp.float32
BF16 = jnp.bfloat16
PIECES = 3
LIMIT = 24 * 1024 * 1024
LIGHT = pl.CostEstimate(flops=10**9, bytes_accessed=10**6, transcendentals=0)

TINY = pl.CostEstimate(flops=10**7, bytes_accessed=10**4, transcendentals=0)


def contract(left, right, dim_left, dim_right):
    return lax.dot_general(
        left, right, (((dim_left,), (dim_right,)), ((), ())), preferred_element_type=F32
    )


class Order:
    def __init__(self, first):
        self.last = first

    def ready(self, *values):
        return lax.optimization_barrier((*values, self.last))[:-1]

    def step(self, work, *values):
        result = work(*self.ready(*values))
        self.last = result
        return result

    def send(self, value, axis, pairs, *others):
        return lax.ppermute(self.ready(value, *others)[0], axis, pairs)


def product_kernel(place, left, right, out):
    out[...] = contract(left[...], right[...], 0, 0).astype(BF16)


def product_rows(place, left, right, width, j):
    rows, nvirt = right.shape
    whole_left = left.shape[1] == width
    step = nvirt // 3
    return pl.pallas_call(
        product_kernel,
        grid_spec=pltpu.PrefetchScalarGridSpec(
            num_scalar_prefetch=1,
            grid=(nvirt // step,),
            in_specs=[
                pl.BlockSpec(
                    (rows, width), lambda i, p: (0, 0 if whole_left else p[0] * PIECES + j)
                ),
                pl.BlockSpec((rows, step), lambda i, p: (0, i)),
            ],
            out_specs=pl.BlockSpec((width, step), lambda i, p: (0, i)),
        ),
        out_shape=jax.ShapeDtypeStruct((width, nvirt), BF16),
        compiler_params=pltpu.CompilerParams(vmem_limit_bytes=LIMIT),
        cost_estimate=LIGHT,
        name="slab_product",
    )(place, left, right)


def add_kernel(left, right, out):
    out[...] = (left[...].astype(F32) + right[...].astype(F32)).astype(BF16)


def added(left, right):
    return pl.pallas_call(
        add_kernel,
        out_shape=jax.ShapeDtypeStruct(left.shape, BF16),
        compiler_params=pltpu.CompilerParams(vmem_limit_bytes=LIMIT),
        cost_estimate=LIGHT,
        name="half_sum",
    )(left, right)


def pick_kernel(hop, slabs, place, left, right, *refs):
    out = refs[-1]
    outer = (place[1] == hop) | (place[1] == slabs - 1 - hop)

    @pl.when(outer)
    def _():
        out[...] = right[...]

    @pl.when(jnp.logical_not(outer))
    def _():
        out[...] = left[...]


def picked(place, left, right, hop, slabs, start, rows, before):
    width, nvirt = left.shape
    return pl.pallas_call(
        functools.partial(pick_kernel, hop, slabs),
        grid=(1,),
        in_specs=[pl.BlockSpec(memory_space=pltpu.SMEM)]
        + [pl.BlockSpec((width, nvirt), lambda i: (0, 0))] * 2
        + [pl.BlockSpec(memory_space=pl.ANY)] * len(before),
        out_specs=pl.BlockSpec((width, nvirt), lambda i: (start // width, 0)),
        out_shape=jax.ShapeDtypeStruct((rows, nvirt), BF16),
        input_output_aliases={3: 0} if before else {},
        compiler_params=pltpu.CompilerParams(vmem_limit_bytes=LIMIT),
        cost_estimate=LIGHT,
        name="amp_of_slab",
    )(place, left, right, *before)


def amp_kernel(place, energy, eps_rows, eps_cols, left, right, out):
    denom = eps_rows[...] + eps_cols[...] - energy[0] - energy[1]
    out[...] = ((left[...].astype(F32) + right[...].astype(F32)) / denom).astype(BF16)


def amplitude(place, energy, eps_rows, eps_cols, left, right, start, half):
    width, nvirt = left.shape
    return pl.pallas_call(
        amp_kernel,
        grid_spec=pltpu.PrefetchScalarGridSpec(
            num_scalar_prefetch=1,
            grid=(1,),
            in_specs=[
                pl.BlockSpec(memory_space=pltpu.SMEM),
                pl.BlockSpec((width, 1), lambda i, p: (p[0] * (half // width) + start // width, 0)),
                pl.BlockSpec((1, nvirt), lambda i, p: (0, 0)),
                pl.BlockSpec((width, nvirt), lambda i, p: (0, 0)),
                pl.BlockSpec((width, nvirt), lambda i, p: (0, 0)),
            ],
            out_specs=pl.BlockSpec((width, nvirt), lambda i, p: (0, 0)),
        ),
        out_shape=jax.ShapeDtypeStruct(left.shape, BF16),
        compiler_params=pltpu.CompilerParams(vmem_limit_bytes=LIMIT),
        cost_estimate=LIGHT,
        name="amplitude",
    )(place, energy, eps_rows, eps_cols, left, right)


def mix_kernel(half, band, rows, cols, straight_core, place, *refs):
    own, other, mix, dens, amp_t, amp, sems = refs
    core, slab, chip = place[0], place[1], place[2]
    nvirt = 2 * half
    step = pl.program_id(0)

    @pl.when(step == 0)
    def _():
        copies = []
        for i, (piece, side) in enumerate(((own, core), (other, 1 - core))):
            start = pl.multiple_of(side * half, 128)
            copies.append(pltpu.make_async_copy(piece, amp_t.at[pl.ds(start, half), :], sems.at[i]))
        for copy in copies:
            copy.start()
        for copy in copies:
            copy.wait()

    straight = core == straight_core
    here = jnp.where(straight, 2.0, -1.0).astype(F32)
    there = jnp.where(straight, -1.0, 2.0).astype(F32)
    start = pl.multiple_of(step * band, band)
    for j in range(nvirt // band):
        tile = amp_t[pl.ds(start, band), j * band : (j + 1) * band].astype(F32)
        turned = amp_t[j * band : (j + 1) * band, pl.ds(start, band)].astype(F32).T
        amp[pl.ds(start, band), j * band : (j + 1) * band] = turned.astype(BF16)
        mix[:, j * band : (j + 1) * band] = (here * tile + there * turned).astype(BF16)

    @pl.when(step == nvirt // band - 1)
    def _():
        chips = dens.shape[0]
        left = amp[pl.ds(pl.multiple_of(slab * rows, rows), rows), :]
        for ahead in range(chips):
            at = pl.multiple_of((2 * lax.rem(chip + ahead, chips) + core) * cols, cols)
            tilde = 2.0 * amp[pl.ds(at, cols), :].astype(F32) - amp_t[pl.ds(at, cols), :].astype(F32)
            dens[ahead] = contract(left, tilde.astype(BF16), 1, 1)


def mix(place, own, other, straight_core, slabs, count):
    nvirt = own.shape[1]
    rows, cols, chips = nvirt // slabs, nvirt // count, count // 2
    band = 256
    return pl.pallas_call(
        functools.partial(mix_kernel, nvirt // 2, band, rows, cols, straight_core),
        grid_spec=pltpu.PrefetchScalarGridSpec(
            num_scalar_prefetch=1,
            grid=(nvirt // band,),
            in_specs=[pl.BlockSpec(memory_space=pl.ANY)] * 2,
            out_specs=[
                pl.BlockSpec((band, nvirt), lambda i, p: (i, 0)),
                pl.BlockSpec((chips, rows, cols), lambda i, p: (0, 0, 0)),
            ],
            scratch_shapes=[
                pltpu.VMEM((nvirt, nvirt), BF16),
                pltpu.VMEM((nvirt, nvirt), BF16),
                pltpu.SemaphoreType.DMA((2,)),
            ],
        ),
        out_shape=[
            jax.ShapeDtypeStruct((nvirt, nvirt), BF16),
            jax.ShapeDtypeStruct((chips, rows, cols), F32),
        ],
        compiler_params=pltpu.CompilerParams(vmem_limit_bytes=LIMIT),
        cost_estimate=TINY,
        name="mix",
    )(place, own, other)


def block_of(rows):
    return 768 if rows % 768 == 0 else 128


def cross_kernel(place, lower, upper, partner, weight, out):
    half = lower.shape[1]

    @pl.when(place[0] == 0)
    def _():
        total = contract(lower[...], weight[:half, :], 1, 0)
        out[...] = (total + contract(upper[...], weight[half:, :], 1, 0)).astype(BF16)

    @pl.when(place[0] != 0)
    def _():
        out[...] = contract(partner[...], weight[...], 1, 0).astype(BF16)


def cross_columns(place, lower, upper, partner, weight, start, step):
    rows, nvirt = partner.shape
    block = block_of(rows)
    return pl.pallas_call(
        cross_kernel,
        grid_spec=pltpu.PrefetchScalarGridSpec(
            num_scalar_prefetch=1,
            grid=(rows // block,),
            in_specs=[
                pl.BlockSpec((block, nvirt // 2), lambda i, p: (jnp.where(p[0] == 0, i, 0), 0)),
                pl.BlockSpec((block, nvirt // 2), lambda i, p: (jnp.where(p[0] == 0, i, 0), 0)),
                pl.BlockSpec((block, nvirt), lambda i, p: (jnp.where(p[0] == 0, 0, i), 0)),
                pl.BlockSpec((nvirt, step), lambda i, p: (0, start // step)),
            ],
            out_specs=pl.BlockSpec((block, step), lambda i, p: (i, 0)),
        ),
        out_shape=jax.ShapeDtypeStruct((rows, step), BF16),
        compiler_params=pltpu.CompilerParams(vmem_limit_bytes=LIMIT),
        cost_estimate=TINY,
        name="cross_term",
    )(place, lower, upper, partner, weight)


def final_kernel(place, partner, weight, kept, arrived, *refs):
    out = refs[-1]
    total = contract(partner[...], weight[...], 1, 0)

    @pl.when(place[0] == 0)
    def _():
        out[0] = (total.astype(BF16).astype(F32) + kept[...].astype(F32)).astype(BF16)

    @pl.when(place[0] != 0)
    def _():
        out[0] = (total + arrived[...].astype(F32)).astype(BF16)


def final_columns(place, partner, weight, kept, arrived, start, step, gamma=None):
    rows, nvirt = partner.shape
    block = block_of(rows)
    before = [] if gamma is None else [gamma]
    return pl.pallas_call(
        final_kernel,
        grid_spec=pltpu.PrefetchScalarGridSpec(
            num_scalar_prefetch=1,
            grid=(rows // block,),
            in_specs=[
                pl.BlockSpec((block, nvirt), lambda i, p: (i, 0)),
                pl.BlockSpec((nvirt, step), lambda i, p: (0, start // step)),
                pl.BlockSpec((block, step), lambda i, p: (jnp.where(p[0] == 0, i, 0), 0)),
                pl.BlockSpec((block, step), lambda i, p: (jnp.where(p[0] == 0, 0, i), 0)),
            ]
            + [pl.BlockSpec(memory_space=pl.ANY)] * len(before),
            out_specs=pl.BlockSpec((1, block, step), lambda i, p: (0, i, start // step)),
        ),
        out_shape=jax.ShapeDtypeStruct((1, rows, nvirt), BF16),
        input_output_aliases={5: 0} if before else {},
        compiler_params=pltpu.CompilerParams(vmem_limit_bytes=LIMIT),
        cost_estimate=TINY,
        name="local_term",
    )(place, partner, weight, kept, arrived, *before)


def shards(bmat, eps_occ, eps_vir, occ_label):
    count = lax.axis_size("occ")
    slabs = lax.axis_size("aux")
    place = lax.axis_index("occ")
    slab_index = lax.axis_index("aux")
    chips = count // 2
    chip, core = place // 2, place % 2
    first = core == 0
    where = jnp.stack([core, slab_index, chip]).astype(jnp.int32)
    nvirt = eps_vir.shape[0]
    half = nvirt // 2
    width = half // PIECES
    labels = jnp.arange(count, dtype=jnp.int32)
    energy = jnp.sum(
        eps_occ[None, :] * (occ_label[:, None] == labels[None, :]).astype(F32), axis=1
    )
    swap_pairs = [(i, i ^ 1) for i in range(count)]
    next_pairs = [(i, (i + 2) % count) for i in range(count)]
    down_pairs = [(i, i - 1) for i in range(1, count, 2)]
    back_pairs = [(i, (i - 2) % count) for i in range(1, count, 2)]

    def energy_at(row):
        return lax.dynamic_index_in_dim(energy, (row + count) % count, 0, keepdims=False)

    energies = {
        "cross": jnp.stack([energy_at(2 * chip), energy_at(2 * chip - 1)]),
        "local": jnp.stack([energy_at(2 * chip + 1), energy_at(2 * chip)]),
    }
    eps_rows, eps_cols = eps_vir.reshape(nvirt, 1), eps_vir.reshape(1, nvirt)

    mine = bmat[0]
    partner = lax.ppermute(mine, "occ", swap_pairs)
    order = Order(partner)
    incoming = {}

    def ship(j, *others):
        sent = order.step(
            lambda p, m: jnp.where(
                first,
                p[:, j * width : (j + 1) * width],
                m[:, half + j * width : half + (j + 1) * width],
            ),
            partner,
            mine,
        )
        incoming[j] = order.send(sent, "occ", next_pairs, *others)

    ship(0)
    odd = order.step(lambda m, p: jnp.where(first, p, m), mine, partner)
    even = order.step(lambda m, p: jnp.where(first, m, p), mine, partner)
    ship(1)

    def product(kind, j):
        if kind == "cross":
            part = order.step(lambda a, b: product_rows(where, a, b, width, j), incoming[j], even)
            if j + 2 < PIECES:
                ship(j + 2)
            return part
        return order.step(lambda a, b: product_rows(where, a, b, width, j), even, odd)

    def scaled(kind, j, mine_sum, other_sum):
        return amplitude(
            where, energies[kind], eps_rows, eps_cols, mine_sum, other_sum, j * width, half
        )

    jobs = [("local", 0)] + [("cross", j) for j in range(PIECES)] + [("local", j) for j in range(1, PIECES)]
    n = len(jobs)
    left = {kind: sum(job[0] == kind for job in jobs) for kind in ("cross", "local")}
    own = {"cross": [], "local": []}
    part, inward, summed, across, amp, outward = ({} for _ in range(6))

    def settle(*values):
        order.last = (order.last, *values)

    hops = slabs // 2 - 1
    middle = [(hops, hops + 1), (hops + 1, hops)]

    def towards_middle(hop):
        return [(hop, hop + 1), (slabs - 1 - hop, slabs - 2 - hop)]

    def towards_ends(hop):
        return [(b, a) for a, b in towards_middle(hop)]

    def feed(s):
        value = product(*jobs[s])
        for hop in range(hops - 1):
            value = order.step(added, value, order.send(value, "aux", towards_middle(hop)))
        part[s] = value
        inward[s] = order.send(value, "aux", towards_middle(hops - 1))

    def pass_across(s):
        if 0 <= s < n:
            summed[s] = order.step(added, part[s], inward[s])
            across[s] = order.send(summed[s], "aux", middle)

    def pass_out(s):
        if 0 <= s < n:
            value = order.step(lambda a, b: scaled(*jobs[s], a, b), summed[s], across[s])
            for hop in reversed(range(1, hops)):
                value = order.step(
                    lambda a, b: picked(where, a, b, hop, slabs, 0, width, ()),
                    value, order.send(value, "aux", towards_ends(hop)),
                )
            amp[s] = value
            outward[s] = order.send(value, "aux", towards_ends(0))

    def collect(s):
        if 0 <= s < n:
            kind, j = jobs[s]
            own[kind] = [
                order.step(
                    lambda a, b, *c: picked(where, a, b, 0, slabs, j * width, half, c), amp[s], outward[s], *own[kind]
                )
            ]
            left[kind] -= 1

    third = nvirt // 3
    spans = [(0, 2 * third), (2 * third, third)]
    kept, arrived = [], []

    def cross_term():
        j = len(kept)
        if j < len(spans) and cross_mix:
            kept.append(
                order.step(
                    lambda w, p, a, b: cross_columns(where, a, b, p, w, *spans[j]),
                    cross_mix[0], partner, received, upper,
                )
            )
            arrived.append(order.send(kept[j], "occ", back_pairs))

    cross_mix = []
    received = upper = None
    for s in range(-1, n + 2):
        if s + 1 < n:
            feed(s + 1)
        pass_across(s)
        if s < n:
            pass_out(s - 1)
            collect(s - 2)
        elif s == n:
            collect(s - 2)
            pass_out(s - 1)
            cross_term()
        else:
            settle(arrived[0])
            collect(s - 2)
        if not left["cross"] and not cross_mix:
            other = order.send(own["cross"][0], "occ", swap_pairs)
            received = order.step(lambda *v: jnp.concatenate(v, axis=1), *incoming.values())
            upper = order.send(received, "occ", down_pairs)
            cross_mix = order.step(lambda a, b: mix(where, a, b, 0, slabs, count), own["cross"][0], other)
            cross_term()
    other = order.send(own["local"][0], "occ", swap_pairs)
    weight, dens = order.step(lambda a, b: mix(where, a, b, 1, slabs, count), own["local"][0], other)
    total = order.step(lambda a, b: (a + b) * nvirt ** (-0.5), cross_mix[1], dens)
    density = total[0]
    for ahead in range(1, chips):
        pairs = [(i, (i + 2 * ahead) % count) for i in range(count)]
        density = density + order.send(total[ahead].astype(BF16), "occ", pairs).astype(F32)
    gamma = None
    for j in range(len(spans)):
        gamma = order.step(
            lambda p, w, k, a, *g: final_columns(where, p, w, k, a, *spans[j], *g),
            partner, weight, kept[j], arrived[j], *([] if gamma is None else [gamma]),
        )
    return gamma, density


def solution(mesh):
    return jax.shard_map(
        shards,
        mesh=mesh,
        in_specs=(P(("grp", "occ"), "aux", None), P("grp"), P("grp"), P("grp")),
        out_specs=(P(("grp", "occ"), "aux", None), P(("grp", "aux"), "occ")),
        check_vma=False,
    )
```

```python
import functools

import jax
import jax.numpy as jnp
from jax import lax
from jax.experimental import pallas as pl
from jax.experimental.pallas import tpu as pltpu
from jax.sharding import PartitionSpec as P

F32 = jnp.float32
BF16 = jnp.bfloat16
PIECES = 3
LIMIT = 24 * 1024 * 1024
LIGHT = pl.CostEstimate(flops=10**9, bytes_accessed=10**6, transcendentals=0)

TINY = pl.CostEstimate(flops=10**7, bytes_accessed=10**4, transcendentals=0)


def contract(left, right, dim_left, dim_right):
    return lax.dot_general(
        left, right, (((dim_left,), (dim_right,)), ((), ())), preferred_element_type=F32
    )


class Order:
    def __init__(self, first):
        self.last = first

    def ready(self, *values):
        return lax.optimization_barrier((*values, self.last))[:-1]

    def step(self, work, *values):
        result = work(*self.ready(*values))
        self.last = result
        return result

    def send(self, value, axis, pairs, *others):
        return lax.ppermute(self.ready(value, *others)[0], axis, pairs)


def product_kernel(place, left, right, out):
    out[...] = contract(left[...], right[...], 0, 0).astype(BF16)


def product_rows(place, left, right, width, j):
    rows, nvirt = right.shape
    whole_left = left.shape[1] == width
    step = nvirt // 3
    return pl.pallas_call(
        product_kernel,
        grid_spec=pltpu.PrefetchScalarGridSpec(
            num_scalar_prefetch=1,
            grid=(nvirt // step,),
            in_specs=[
                pl.BlockSpec(
                    (rows, width), lambda i, p: (0, 0 if whole_left else p[0] * PIECES + j)
                ),
                pl.BlockSpec((rows, step), lambda i, p: (0, i)),
            ],
            out_specs=pl.BlockSpec((width, step), lambda i, p: (0, i)),
        ),
        out_shape=jax.ShapeDtypeStruct((width, nvirt), BF16),
        compiler_params=pltpu.CompilerParams(vmem_limit_bytes=LIMIT),
        cost_estimate=LIGHT,
        name="slab_product",
    )(place, left, right)


def add_kernel(left, right, out):
    out[...] = (left[...].astype(F32) + right[...].astype(F32)).astype(BF16)


def added(left, right):
    return pl.pallas_call(
        add_kernel,
        out_shape=jax.ShapeDtypeStruct(left.shape, BF16),
        compiler_params=pltpu.CompilerParams(vmem_limit_bytes=LIMIT),
        cost_estimate=LIGHT,
        name="half_sum",
    )(left, right)


def pick_kernel(hop, slabs, place, left, right, *refs):
    out = refs[-1]
    outer = (place[1] == hop) | (place[1] == slabs - 1 - hop)

    @pl.when(outer)
    def _():
        out[...] = right[...]

    @pl.when(jnp.logical_not(outer))
    def _():
        out[...] = left[...]


def picked(place, left, right, hop, slabs, start, rows, before):
    width, nvirt = left.shape
    return pl.pallas_call(
        functools.partial(pick_kernel, hop, slabs),
        grid=(1,),
        in_specs=[pl.BlockSpec(memory_space=pltpu.SMEM)]
        + [pl.BlockSpec((width, nvirt), lambda i: (0, 0))] * 2
        + [pl.BlockSpec(memory_space=pl.ANY)] * len(before),
        out_specs=pl.BlockSpec((width, nvirt), lambda i: (start // width, 0)),
        out_shape=jax.ShapeDtypeStruct((rows, nvirt), BF16),
        input_output_aliases={3: 0} if before else {},
        compiler_params=pltpu.CompilerParams(vmem_limit_bytes=LIMIT),
        cost_estimate=LIGHT,
        name="amp_of_slab",
    )(place, left, right, *before)


def amp_kernel(place, energy, eps_rows, eps_cols, left, right, out):
    denom = eps_rows[...] + eps_cols[...] - energy[0] - energy[1]
    out[...] = ((left[...].astype(F32) + right[...].astype(F32)) / denom).astype(BF16)


def amplitude(place, energy, eps_rows, eps_cols, left, right, start, half):
    width, nvirt = left.shape
    return pl.pallas_call(
        amp_kernel,
        grid_spec=pltpu.PrefetchScalarGridSpec(
            num_scalar_prefetch=1,
            grid=(1,),
            in_specs=[
                pl.BlockSpec(memory_space=pltpu.SMEM),
                pl.BlockSpec((width, 1), lambda i, p: (p[0] * (half // width) + start // width, 0)),
                pl.BlockSpec((1, nvirt), lambda i, p: (0, 0)),
                pl.BlockSpec((width, nvirt), lambda i, p: (0, 0)),
                pl.BlockSpec((width, nvirt), lambda i, p: (0, 0)),
            ],
            out_specs=pl.BlockSpec((width, nvirt), lambda i, p: (0, 0)),
        ),
        out_shape=jax.ShapeDtypeStruct(left.shape, BF16),
        compiler_params=pltpu.CompilerParams(vmem_limit_bytes=LIMIT),
        cost_estimate=LIGHT,
        name="amplitude",
    )(place, energy, eps_rows, eps_cols, left, right)


def mix_kernel(half, band, rows, cols, straight_core, place, *refs):
    own, *other, mix, dens, amp_t, amp, sems = refs
    core, slab, chip = place[0], place[1], place[2]
    nvirt = 2 * half
    step = pl.program_id(0)

    @pl.when(step == 0)
    def _():
        copies = []
        for i, piece in enumerate((own, *other)):
            width = piece.shape[0]
            start = core * half if i == 0 else (1 - core) * half + (i - 1) * width
            rows_at = pl.ds(pl.multiple_of(start, 128), width)
            copies.append(pltpu.make_async_copy(piece, amp_t.at[rows_at, :], sems.at[i]))
        for copy in copies:
            copy.start()
        for copy in copies:
            copy.wait()

    straight = core == straight_core
    here = jnp.where(straight, 2.0, -1.0).astype(F32)
    there = jnp.where(straight, -1.0, 2.0).astype(F32)
    start = pl.multiple_of(step * band, band)
    for j in range(nvirt // band):
        tile = amp_t[pl.ds(start, band), j * band : (j + 1) * band].astype(F32)
        turned = amp_t[j * band : (j + 1) * band, pl.ds(start, band)].astype(F32).T
        amp[pl.ds(start, band), j * band : (j + 1) * band] = turned.astype(BF16)
        mix[:, j * band : (j + 1) * band] = (here * tile + there * turned).astype(BF16)

    @pl.when(step == nvirt // band - 1)
    def _():
        chips = dens.shape[0]
        left = amp[pl.ds(pl.multiple_of(slab * rows, rows), rows), :]
        for ahead in range(chips):
            at = pl.multiple_of((2 * lax.rem(chip + ahead, chips) + core) * cols, cols)
            tilde = 2.0 * amp[pl.ds(at, cols), :].astype(F32) - amp_t[pl.ds(at, cols), :].astype(F32)
            dens[ahead] = contract(left, tilde.astype(BF16), 1, 1)


def mix(place, own, other, straight_core, slabs, count):
    nvirt = own.shape[1]
    rows, cols, chips = nvirt // slabs, nvirt // count, count // 2
    band = 256
    return pl.pallas_call(
        functools.partial(mix_kernel, nvirt // 2, band, rows, cols, straight_core),
        grid_spec=pltpu.PrefetchScalarGridSpec(
            num_scalar_prefetch=1,
            grid=(nvirt // band,),
            in_specs=[pl.BlockSpec(memory_space=pl.ANY)] * (1 + len(other)),
            out_specs=[
                pl.BlockSpec((band, nvirt), lambda i, p: (i, 0)),
                pl.BlockSpec((chips, rows, cols), lambda i, p: (0, 0, 0)),
            ],
            scratch_shapes=[
                pltpu.VMEM((nvirt, nvirt), BF16),
                pltpu.VMEM((nvirt, nvirt), BF16),
                pltpu.SemaphoreType.DMA((1 + len(other),)),
            ],
        ),
        out_shape=[
            jax.ShapeDtypeStruct((nvirt, nvirt), BF16),
            jax.ShapeDtypeStruct((chips, rows, cols), F32),
        ],
        compiler_params=pltpu.CompilerParams(vmem_limit_bytes=LIMIT),
        cost_estimate=TINY,
        name="mix",
    )(place, own, *other)


def block_of(rows):
    return 768 if rows % 768 == 0 else 128


def cross_kernel(place, lower, upper, partner, weight, out):
    half = lower.shape[1]

    @pl.when(place[0] == 0)
    def _():
        total = contract(lower[...], weight[:half, :], 1, 0)
        out[...] = (total + contract(upper[...], weight[half:, :], 1, 0)).astype(BF16)

    @pl.when(place[0] != 0)
    def _():
        out[...] = contract(partner[...], weight[...], 1, 0).astype(BF16)


def cross_columns(place, lower, upper, partner, weight, start, step):
    rows, nvirt = partner.shape
    block = block_of(rows)
    part = nvirt // 3
    return pl.pallas_call(
        cross_kernel,
        grid_spec=pltpu.PrefetchScalarGridSpec(
            num_scalar_prefetch=1,
            grid=(step // part, rows // block),
            in_specs=[
                pl.BlockSpec((block, nvirt // 2), lambda j, i, p: (jnp.where(p[0] == 0, i, 0), 0)),
                pl.BlockSpec((block, nvirt // 2), lambda j, i, p: (jnp.where(p[0] == 0, i, 0), 0)),
                pl.BlockSpec((block, nvirt), lambda j, i, p: (jnp.where(p[0] == 0, 0, i), 0)),
                pl.BlockSpec((nvirt, part), lambda j, i, p: (0, start // part + j)),
            ],
            out_specs=pl.BlockSpec((block, part), lambda j, i, p: (i, j)),
        ),
        out_shape=jax.ShapeDtypeStruct((rows, step), BF16),
        compiler_params=pltpu.CompilerParams(vmem_limit_bytes=LIMIT),
        cost_estimate=TINY,
        name="cross_term",
    )(place, lower, upper, partner, weight)


def final_kernel(place, partner, weight, kept, arrived, *refs):
    out = refs[-1]
    total = contract(partner[...], weight[...], 1, 0)

    @pl.when(place[0] == 0)
    def _():
        out[0] = (total.astype(BF16).astype(F32) + kept[...].astype(F32)).astype(BF16)

    @pl.when(place[0] != 0)
    def _():
        out[0] = (total + arrived[...].astype(F32)).astype(BF16)


def final_columns(place, partner, weight, kept, arrived, start, step, gamma=None):
    rows, nvirt = partner.shape
    block = block_of(rows)
    before = [] if gamma is None else [gamma]
    return pl.pallas_call(
        final_kernel,
        grid_spec=pltpu.PrefetchScalarGridSpec(
            num_scalar_prefetch=1,
            grid=(rows // block,),
            in_specs=[
                pl.BlockSpec((block, nvirt), lambda i, p: (i, 0)),
                pl.BlockSpec((nvirt, step), lambda i, p: (0, start // step)),
                pl.BlockSpec((block, step), lambda i, p: (jnp.where(p[0] == 0, i, 0), 0)),
                pl.BlockSpec((block, step), lambda i, p: (jnp.where(p[0] == 0, 0, i), 0)),
            ]
            + [pl.BlockSpec(memory_space=pl.ANY)] * len(before),
            out_specs=pl.BlockSpec((1, block, step), lambda i, p: (0, i, start // step)),
        ),
        out_shape=jax.ShapeDtypeStruct((1, rows, nvirt), BF16),
        input_output_aliases={5: 0} if before else {},
        compiler_params=pltpu.CompilerParams(vmem_limit_bytes=LIMIT),
        cost_estimate=TINY,
        name="local_term",
    )(place, partner, weight, kept, arrived, *before)


def local_kernel(partner, weight, out):
    out[...] = contract(partner[...], weight[...], 1, 0).astype(BF16)


def local_columns(partner, weight, start, step):
    rows, nvirt = partner.shape
    block = block_of(rows)
    part = nvirt // 3
    return pl.pallas_call(
        local_kernel,
        grid=(step // part, rows // block),
        in_specs=[
            pl.BlockSpec((block, nvirt), lambda j, i: (i, 0)),
            pl.BlockSpec((nvirt, part), lambda j, i: (0, start // part + j)),
        ],
        out_specs=pl.BlockSpec((block, part), lambda j, i: (i, j)),
        out_shape=jax.ShapeDtypeStruct((rows, step), BF16),
        compiler_params=pltpu.CompilerParams(vmem_limit_bytes=LIMIT),
        cost_estimate=TINY,
        name="local_rest",
    )(partner, weight)


def closing_kernel(place, rest, kept, arrived, gamma, out):
    @pl.when(place[0] == 0)
    def _():
        out[0] = (rest[...].astype(F32) + kept[...].astype(F32)).astype(BF16)

    @pl.when(place[0] != 0)
    def _():
        out[0] = (rest[...].astype(F32) + arrived[...].astype(F32)).astype(BF16)


def closing_columns(place, rest, kept, arrived, start, step, gamma):
    rows = rest.shape[0]
    part = 256
    return pl.pallas_call(
        closing_kernel,
        grid_spec=pltpu.PrefetchScalarGridSpec(
            num_scalar_prefetch=1,
            grid=(step // part,),
            in_specs=[
                pl.BlockSpec((rows, part), lambda i, p: (0, i)),
                pl.BlockSpec((rows, part), lambda i, p: (0, jnp.where(p[0] == 0, i, 0))),
                pl.BlockSpec((rows, part), lambda i, p: (0, jnp.where(p[0] == 0, 0, i))),
                pl.BlockSpec(memory_space=pl.ANY),
            ],
            out_specs=pl.BlockSpec((1, rows, part), lambda i, p: (0, 0, start // part + i)),
        ),
        out_shape=jax.ShapeDtypeStruct(gamma.shape, BF16),
        input_output_aliases={4: 0},
        compiler_params=pltpu.CompilerParams(vmem_limit_bytes=LIMIT),
        cost_estimate=TINY,
        name="closing_sum",
    )(place, rest, kept, arrived, gamma)


def shards(bmat, eps_occ, eps_vir, occ_label):
    count = lax.axis_size("occ")
    slabs = lax.axis_size("aux")
    place = lax.axis_index("occ")
    slab_index = lax.axis_index("aux")
    chips = count // 2
    chip, core = place // 2, place % 2
    first = core == 0
    where = jnp.stack([core, slab_index, chip]).astype(jnp.int32)
    nvirt = eps_vir.shape[0]
    half = nvirt // 2
    width = half // PIECES
    labels = jnp.arange(count, dtype=jnp.int32)
    energy = jnp.sum(
        eps_occ[None, :] * (occ_label[:, None] == labels[None, :]).astype(F32), axis=1
    )
    swap_pairs = [(i, i ^ 1) for i in range(count)]
    next_pairs = [(i, (i + 2) % count) for i in range(count)]
    down_pairs = [(i, i - 1) for i in range(1, count, 2)]
    back_pairs = [(i, (i - 2) % count) for i in range(1, count, 2)]

    def energy_at(row):
        return lax.dynamic_index_in_dim(energy, (row + count) % count, 0, keepdims=False)

    energies = {
        "cross": jnp.stack([energy_at(2 * chip), energy_at(2 * chip - 1)]),
        "local": jnp.stack([energy_at(2 * chip + 1), energy_at(2 * chip)]),
    }
    eps_rows, eps_cols = eps_vir.reshape(nvirt, 1), eps_vir.reshape(1, nvirt)

    mine = bmat[0]
    order = Order(where)
    incoming = {}

    def ship(j, low, high):
        sent = order.step(lambda a, b: jnp.where(first, a, b), low, high)
        incoming[j] = order.send(sent, "occ", next_pairs)

    def columns(value, start):
        return lax.slice_in_dim(value, start, start + width, axis=1)

    ship(0, order.send(columns(mine, 0), "occ", down_pairs), columns(mine, half))
    partner = order.send(mine, "occ", swap_pairs)
    ship(1, columns(partner, width), columns(mine, half + width))
    odd = order.step(lambda m, p: jnp.where(first, p, m), mine, partner)
    even = order.step(lambda m, p: jnp.where(first, m, p), mine, partner)

    def product(kind, j):
        if kind == "cross":
            part = order.step(lambda a, b: product_rows(where, a, b, width, j), incoming[j], even)
            if j + 2 < PIECES:
                ship(j + 2, columns(partner, (j + 2) * width), columns(mine, half + (j + 2) * width))
            return part
        return order.step(lambda a, b: product_rows(where, a, b, width, j), even, odd)

    def scaled(kind, j, mine_sum, other_sum):
        return amplitude(
            where, energies[kind], eps_rows, eps_cols, mine_sum, other_sum, j * width, half
        )

    jobs = [("local", 0), ("cross", 0), ("cross", 1), ("cross", 2), ("local", 1), ("local", 2)]
    n = len(jobs)
    left = {kind: sum(job[0] == kind for job in jobs) for kind in ("cross", "local")}
    own = {"cross": [], "local": []}
    part, inward, summed, across, amp, outward = ({} for _ in range(6))

    def settle(*values):
        order.last = (order.last, *values)

    hops = slabs // 2 - 1
    middle = [(hops, hops + 1), (hops + 1, hops)]

    def towards_middle(hop):
        return [(hop, hop + 1), (slabs - 1 - hop, slabs - 2 - hop)]

    def towards_ends(hop):
        return [(b, a) for a, b in towards_middle(hop)]

    def feed(s):
        value = product(*jobs[s])
        for hop in range(hops - 1):
            value = order.step(added, value, order.send(value, "aux", towards_middle(hop)))
        part[s] = value
        inward[s] = order.send(value, "aux", towards_middle(hops - 1))

    def pass_across(s):
        if 0 <= s < n:
            summed[s] = order.step(added, part[s], inward[s])
            across[s] = order.send(summed[s], "aux", middle)

    def pass_out(s):
        if 0 <= s < n:
            value = order.step(lambda a, b: scaled(*jobs[s], a, b), summed[s], across[s])
            for hop in reversed(range(1, hops)):
                value = order.step(
                    lambda a, b: picked(where, a, b, hop, slabs, 0, width, ()),
                    value, order.send(value, "aux", towards_ends(hop)),
                )
            amp[s] = value
            outward[s] = order.send(value, "aux", towards_ends(0))

    def collect(s):
        if 0 <= s < n:
            kind, j = jobs[s]
            own[kind] = [
                order.step(
                    lambda a, b, *c: picked(where, a, b, 0, slabs, j * width, half, c), amp[s], outward[s], *own[kind]
                )
            ]
            left[kind] -= 1

    third = nvirt // 3
    spans = [(0, third), (third, 2 * third)]
    kept, arrived = [], []

    def cross_term():
        j = len(kept)
        if j < len(spans) and cross_mix:
            kept.append(
                order.step(
                    lambda w, p, a, b: cross_columns(where, a, b, p, w, *spans[j]),
                    cross_mix[0], partner, received, upper,
                )
            )
            arrived.append(order.send(kept[j], "occ", back_pairs))

    cross_mix = []
    for s in range(-1, n + 2):
        if s + 1 < n:
            feed(s + 1)
        pass_across(s)
        if not cross_mix:
            pass_out(s - 1)
            collect(s - 2)
        else:
            if s == n + 1:
                settle(arrived[0])
            collect(s - 2)
            pass_out(s - 1)
            cross_term()
        if not left["cross"] and not cross_mix:
            other = order.send(own["cross"][0], "occ", swap_pairs)
            received = order.step(lambda *v: jnp.concatenate(v, axis=1), *incoming.values())
            upper = order.send(received, "occ", down_pairs)
            cross_mix = order.step(
                lambda a, b: mix(where, a, (b,), 0, slabs, count), own["cross"][0], other
            )
            cross_term()
    while len(kept) < len(spans):
        cross_term()

    other = [
        order.send(lax.slice_in_dim(own["local"][0], j * width, (j + 1) * width), "occ", swap_pairs)
        for j in range(PIECES)
    ]
    weight, dens = order.step(
        lambda a, *b: mix(where, a, b, 1, slabs, count), own["local"][0], *other
    )
    total = order.step(lambda a, b: (a + b) * nvirt ** (-0.5), cross_mix[1], dens)
    density = total[0]
    moved = []
    for ahead in range(1, chips):
        pairs = [(i, (i + 2 * ahead) % count) for i in range(count)]
        moved.append(order.send(total[ahead].astype(BF16), "occ", pairs))
    gamma = order.step(
        lambda p, w, k, a: final_columns(where, p, w, k, a, *spans[0]), partner, weight, kept[0], arrived[0]
    )
    rest = order.step(lambda p, w: local_columns(p, w, *spans[1]), partner, weight)
    gamma = order.step(
        lambda r, k, a, g: closing_columns(where, r, k, a, *spans[1], g), rest, kept[1], arrived[1], gamma
    )
    density = order.step(lambda d, *m: d + sum(v.astype(F32) for v in m), density, *moved)
    return gamma, density


def solution(mesh):
    return jax.shard_map(
        shards,
        mesh=mesh,
        in_specs=(P(("grp", "occ"), "aux", None), P("grp"), P("grp"), P("grp")),
        out_specs=(P(("grp", "occ"), "aux", None), P(("grp", "aux"), "occ")),
        check_vma=False,
    )
```

```python
import functools

import jax
import jax.numpy as jnp
from jax import lax
from jax.experimental import pallas as pl
from jax.experimental.pallas import tpu as pltpu
from jax.sharding import PartitionSpec as P

F32 = jnp.float32
BF16 = jnp.bfloat16
PIECES = 3
LIMIT = 24 * 1024 * 1024
LIGHT = pl.CostEstimate(flops=10**9, bytes_accessed=10**6, transcendentals=0)

TINY = pl.CostEstimate(flops=10**7, bytes_accessed=10**4, transcendentals=0)


def contract(left, right, dim_left, dim_right):
    return lax.dot_general(
        left, right, (((dim_left,), (dim_right,)), ((), ())), preferred_element_type=F32
    )


class Order:
    def __init__(self, first):
        self.last = first

    def ready(self, *values):
        return lax.optimization_barrier((*values, self.last))[:-1]

    def step(self, work, *values):
        result = work(*self.ready(*values))
        self.last = result
        return result

    def send(self, value, axis, pairs, *others):
        return lax.ppermute(self.ready(value, *others)[0], axis, pairs)


def product_kernel(place, left, right, out):
    out[...] = contract(left[...], right[...], 0, 0).astype(BF16)


def product_rows(place, left, right, width, j):
    rows, nvirt = right.shape
    whole_left = left.shape[1] == width
    step = nvirt // 3
    return pl.pallas_call(
        product_kernel,
        grid_spec=pltpu.PrefetchScalarGridSpec(
            num_scalar_prefetch=1,
            grid=(nvirt // step,),
            in_specs=[
                pl.BlockSpec(
                    (rows, width), lambda i, p: (0, 0 if whole_left else p[0] * PIECES + j)
                ),
                pl.BlockSpec((rows, step), lambda i, p: (0, i)),
            ],
            out_specs=pl.BlockSpec((width, step), lambda i, p: (0, i)),
        ),
        out_shape=jax.ShapeDtypeStruct((width, nvirt), BF16),
        compiler_params=pltpu.CompilerParams(vmem_limit_bytes=LIMIT),
        cost_estimate=LIGHT,
        name="slab_product",
    )(place, left, right)


def add_kernel(left, right, out):
    out[...] = (left[...].astype(F32) + right[...].astype(F32)).astype(BF16)


def added(left, right):
    return pl.pallas_call(
        add_kernel,
        out_shape=jax.ShapeDtypeStruct(left.shape, BF16),
        compiler_params=pltpu.CompilerParams(vmem_limit_bytes=LIMIT),
        cost_estimate=LIGHT,
        name="half_sum",
    )(left, right)


def pick_kernel(hop, slabs, place, left, right, *refs):
    out = refs[-1]
    outer = (place[1] == hop) | (place[1] == slabs - 1 - hop)

    @pl.when(outer)
    def _():
        out[...] = right[...]

    @pl.when(jnp.logical_not(outer))
    def _():
        out[...] = left[...]


def picked(place, left, right, hop, slabs, start, rows, before):
    width, nvirt = left.shape
    return pl.pallas_call(
        functools.partial(pick_kernel, hop, slabs),
        grid=(1,),
        in_specs=[pl.BlockSpec(memory_space=pltpu.SMEM)]
        + [pl.BlockSpec((width, nvirt), lambda i: (0, 0))] * 2
        + [pl.BlockSpec(memory_space=pl.ANY)] * len(before),
        out_specs=pl.BlockSpec((width, nvirt), lambda i: (start // width, 0)),
        out_shape=jax.ShapeDtypeStruct((rows, nvirt), BF16),
        input_output_aliases={3: 0} if before else {},
        compiler_params=pltpu.CompilerParams(vmem_limit_bytes=LIMIT),
        cost_estimate=LIGHT,
        name="amp_of_slab",
    )(place, left, right, *before)


def amp_kernel(place, energy, eps_rows, eps_cols, left, right, out):
    denom = eps_rows[...] + eps_cols[...] - energy[0] - energy[1]
    out[...] = ((left[...].astype(F32) + right[...].astype(F32)) / denom).astype(BF16)


def amplitude(place, energy, eps_rows, eps_cols, left, right, start, half):
    width, nvirt = left.shape
    return pl.pallas_call(
        amp_kernel,
        grid_spec=pltpu.PrefetchScalarGridSpec(
            num_scalar_prefetch=1,
            grid=(1,),
            in_specs=[
                pl.BlockSpec(memory_space=pltpu.SMEM),
                pl.BlockSpec((width, 1), lambda i, p: (p[0] * (half // width) + start // width, 0)),
                pl.BlockSpec((1, nvirt), lambda i, p: (0, 0)),
                pl.BlockSpec((width, nvirt), lambda i, p: (0, 0)),
                pl.BlockSpec((width, nvirt), lambda i, p: (0, 0)),
            ],
            out_specs=pl.BlockSpec((width, nvirt), lambda i, p: (0, 0)),
        ),
        out_shape=jax.ShapeDtypeStruct(left.shape, BF16),
        compiler_params=pltpu.CompilerParams(vmem_limit_bytes=LIMIT),
        cost_estimate=LIGHT,
        name="amplitude",
    )(place, energy, eps_rows, eps_cols, left, right)


def mix_kernel(owned, half, band, rows, cols, straight_core, place, *refs):
    *pieces, mix, dens, amp_t, amp, sems = refs
    own, other = pieces[:owned], pieces[owned:]
    core, slab, chip = place[0], place[1], place[2]
    nvirt = 2 * half
    step = pl.program_id(0)

    @pl.when(step == 0)
    def _():
        copies = []
        for side, group in ((core, own), (1 - core, other)):
            start = side * half
            for piece in group:
                rows_at = pl.ds(pl.multiple_of(start, 128), piece.shape[0])
                copies.append(pltpu.make_async_copy(piece, amp_t.at[rows_at, :], sems.at[len(copies)]))
                start += piece.shape[0]
        for copy in copies:
            copy.start()
        for copy in copies:
            copy.wait()

    straight = core == straight_core
    here = jnp.where(straight, 2.0, -1.0).astype(F32)
    there = jnp.where(straight, -1.0, 2.0).astype(F32)
    start = pl.multiple_of(step * band, band)
    for j in range(nvirt // band):
        tile = amp_t[pl.ds(start, band), j * band : (j + 1) * band].astype(F32)
        turned = amp_t[j * band : (j + 1) * band, pl.ds(start, band)].astype(F32).T
        amp[pl.ds(start, band), j * band : (j + 1) * band] = turned.astype(BF16)
        mix[:, j * band : (j + 1) * band] = (here * tile + there * turned).astype(BF16)

    @pl.when(step == nvirt // band - 1)
    def _():
        chips = dens.shape[0]
        left = amp[pl.ds(pl.multiple_of(slab * rows, rows), rows), :]
        for ahead in range(chips):
            at = pl.multiple_of((2 * lax.rem(chip + ahead, chips) + core) * cols, cols)
            tilde = 2.0 * amp[pl.ds(at, cols), :].astype(F32) - amp_t[pl.ds(at, cols), :].astype(F32)
            dens[ahead] = contract(left, tilde.astype(BF16), 1, 1)


def mix(place, own, other, straight_core, slabs, count):
    nvirt = own[0].shape[1]
    rows, cols, chips = nvirt // slabs, nvirt // count, count // 2
    band = 256
    return pl.pallas_call(
        functools.partial(mix_kernel, len(own), nvirt // 2, band, rows, cols, straight_core),
        grid_spec=pltpu.PrefetchScalarGridSpec(
            num_scalar_prefetch=1,
            grid=(nvirt // band,),
            in_specs=[pl.BlockSpec(memory_space=pl.ANY)] * (len(own) + len(other)),
            out_specs=[
                pl.BlockSpec((band, nvirt), lambda i, p: (i, 0)),
                pl.BlockSpec((chips, rows, cols), lambda i, p: (0, 0, 0)),
            ],
            scratch_shapes=[
                pltpu.VMEM((nvirt, nvirt), BF16),
                pltpu.VMEM((nvirt, nvirt), BF16),
                pltpu.SemaphoreType.DMA((len(own) + len(other),)),
            ],
        ),
        out_shape=[
            jax.ShapeDtypeStruct((nvirt, nvirt), BF16),
            jax.ShapeDtypeStruct((chips, rows, cols), F32),
        ],
        compiler_params=pltpu.CompilerParams(vmem_limit_bytes=LIMIT),
        cost_estimate=TINY,
        name="mix",
    )(place, *own, *other)


def block_of(rows):
    return 768 if rows % 768 == 0 else 128


def cross_kernel(place, lower, upper, partner, weight, out):
    half = lower.shape[1]

    @pl.when(place[0] == 0)
    def _():
        total = contract(lower[...], weight[:half, :], 1, 0)
        out[...] = (total + contract(upper[...], weight[half:, :], 1, 0)).astype(BF16)

    @pl.when(place[0] != 0)
    def _():
        out[...] = contract(partner[...], weight[...], 1, 0).astype(BF16)


def cross_columns(place, lower, upper, partner, weight, start, step):
    rows, nvirt = partner.shape
    block = block_of(rows)
    part = nvirt // 3
    return pl.pallas_call(
        cross_kernel,
        grid_spec=pltpu.PrefetchScalarGridSpec(
            num_scalar_prefetch=1,
            grid=(step // part, rows // block),
            in_specs=[
                pl.BlockSpec((block, nvirt // 2), lambda j, i, p: (jnp.where(p[0] == 0, i, 0), 0)),
                pl.BlockSpec((block, nvirt // 2), lambda j, i, p: (jnp.where(p[0] == 0, i, 0), 0)),
                pl.BlockSpec((block, nvirt), lambda j, i, p: (jnp.where(p[0] == 0, 0, i), 0)),
                pl.BlockSpec((nvirt, part), lambda j, i, p: (0, start // part + j)),
            ],
            out_specs=pl.BlockSpec((block, part), lambda j, i, p: (i, j)),
        ),
        out_shape=jax.ShapeDtypeStruct((rows, step), BF16),
        compiler_params=pltpu.CompilerParams(vmem_limit_bytes=LIMIT),
        cost_estimate=TINY,
        name="cross_term",
    )(place, lower, upper, partner, weight)


def final_kernel(place, partner, weight, kept, arrived, *refs):
    out = refs[-1]
    total = contract(partner[...], weight[...], 1, 0)

    @pl.when(place[0] == 0)
    def _():
        out[0] = (total.astype(BF16).astype(F32) + kept[...].astype(F32)).astype(BF16)

    @pl.when(place[0] != 0)
    def _():
        out[0] = (total + arrived[...].astype(F32)).astype(BF16)


def final_columns(place, partner, weight, kept, arrived, start, step, gamma=None):
    rows, nvirt = partner.shape
    block = block_of(rows)
    part = nvirt // 3
    before = [] if gamma is None else [gamma]
    return pl.pallas_call(
        final_kernel,
        grid_spec=pltpu.PrefetchScalarGridSpec(
            num_scalar_prefetch=1,
            grid=(step // part, rows // block),
            in_specs=[
                pl.BlockSpec((block, nvirt), lambda j, i, p: (i, 0)),
                pl.BlockSpec((nvirt, part), lambda j, i, p: (0, start // part + j)),
                pl.BlockSpec((block, part), lambda j, i, p: (jnp.where(p[0] == 0, i, 0), jnp.where(p[0] == 0, j, 0))),
                pl.BlockSpec((block, part), lambda j, i, p: (jnp.where(p[0] == 0, 0, i), jnp.where(p[0] == 0, 0, j))),
            ]
            + [pl.BlockSpec(memory_space=pl.ANY)] * len(before),
            out_specs=pl.BlockSpec((1, block, part), lambda j, i, p: (0, i, start // part + j)),
        ),
        out_shape=jax.ShapeDtypeStruct((1, rows, nvirt), BF16),
        input_output_aliases={5: 0} if before else {},
        compiler_params=pltpu.CompilerParams(vmem_limit_bytes=LIMIT),
        cost_estimate=TINY,
        name="local_term",
    )(place, partner, weight, kept, arrived, *before)


def local_kernel(partner, weight, out):
    out[...] = contract(partner[...], weight[...], 1, 0).astype(BF16)


def local_columns(partner, weight, start, step):
    rows, nvirt = partner.shape
    block = block_of(rows)
    part = nvirt // 3
    return pl.pallas_call(
        local_kernel,
        grid=(step // part, rows // block),
        in_specs=[
            pl.BlockSpec((block, nvirt), lambda j, i: (i, 0)),
            pl.BlockSpec((nvirt, part), lambda j, i: (0, start // part + j)),
        ],
        out_specs=pl.BlockSpec((block, part), lambda j, i: (i, j)),
        out_shape=jax.ShapeDtypeStruct((rows, step), BF16),
        compiler_params=pltpu.CompilerParams(vmem_limit_bytes=LIMIT),
        cost_estimate=pl.CostEstimate(flops=5760000000, bytes_accessed=10**4, transcendentals=0),
        name="local_rest",
    )(partner, weight)


def closing_kernel(place, rest, kept, arrived, gamma, out):
    @pl.when(place[0] == 0)
    def _():
        out[0] = (rest[...].astype(F32) + kept[...].astype(F32)).astype(BF16)

    @pl.when(place[0] != 0)
    def _():
        out[0] = (rest[...].astype(F32) + arrived[...].astype(F32)).astype(BF16)


def closing_columns(place, rest, kept, arrived, start, step, gamma):
    rows = rest.shape[0]
    part = 256
    return pl.pallas_call(
        closing_kernel,
        grid_spec=pltpu.PrefetchScalarGridSpec(
            num_scalar_prefetch=1,
            grid=(step // part,),
            in_specs=[
                pl.BlockSpec((rows, part), lambda i, p: (0, i)),
                pl.BlockSpec((rows, part), lambda i, p: (0, jnp.where(p[0] == 0, i, 0))),
                pl.BlockSpec((rows, part), lambda i, p: (0, jnp.where(p[0] == 0, 0, i))),
                pl.BlockSpec(memory_space=pl.ANY),
            ],
            out_specs=pl.BlockSpec((1, rows, part), lambda i, p: (0, 0, start // part + i)),
        ),
        out_shape=jax.ShapeDtypeStruct(gamma.shape, BF16),
        input_output_aliases={4: 0},
        compiler_params=pltpu.CompilerParams(vmem_limit_bytes=LIMIT),
        cost_estimate=TINY,
        name="closing_sum",
    )(place, rest, kept, arrived, gamma)


def shards(bmat, eps_occ, eps_vir, occ_label):
    count = lax.axis_size("occ")
    slabs = lax.axis_size("aux")
    place = lax.axis_index("occ")
    slab_index = lax.axis_index("aux")
    chips = count // 2
    chip, core = place // 2, place % 2
    first = core == 0
    where = jnp.stack([core, slab_index, chip]).astype(jnp.int32)
    nvirt = eps_vir.shape[0]
    half = nvirt // 2
    width = half // PIECES
    labels = jnp.arange(count, dtype=jnp.int32)
    energy = jnp.sum(
        eps_occ[None, :] * (occ_label[:, None] == labels[None, :]).astype(F32), axis=1
    )
    swap_pairs = [(i, i ^ 1) for i in range(count)]
    next_pairs = [(i, (i + 2) % count) for i in range(count)]
    down_pairs = [(i, i - 1) for i in range(1, count, 2)]
    back_pairs = [(i, (i - 2) % count) for i in range(1, count, 2)]

    def energy_at(row):
        return lax.dynamic_index_in_dim(energy, (row + count) % count, 0, keepdims=False)

    energies = {
        "cross": jnp.stack([energy_at(2 * chip), energy_at(2 * chip - 1)]),
        "local": jnp.stack([energy_at(2 * chip + 1), energy_at(2 * chip)]),
    }
    eps_rows, eps_cols = eps_vir.reshape(nvirt, 1), eps_vir.reshape(1, nvirt)

    mine = bmat[0]
    order = Order(where)
    incoming = {}

    def ship(j, low, high):
        sent = order.step(lambda a, b: jnp.where(first, a, b), low, high)
        incoming[j] = order.send(sent, "occ", next_pairs)

    def columns(value, start):
        return lax.slice_in_dim(value, start, start + width, axis=1)

    ship(0, order.send(columns(mine, 0), "occ", down_pairs), columns(mine, half))
    partner = order.send(mine, "occ", swap_pairs)
    ship(1, columns(partner, width), columns(mine, half + width))
    odd = order.step(lambda m, p: jnp.where(first, p, m), mine, partner)
    even = order.step(lambda m, p: jnp.where(first, m, p), mine, partner)

    def product(kind, j):
        if kind == "cross":
            part = order.step(lambda a, b: product_rows(where, a, b, width, j), incoming[j], even)
            if j + 2 < PIECES:
                ship(j + 2, columns(partner, (j + 2) * width), columns(mine, half + (j + 2) * width))
            return part
        return order.step(lambda a, b: product_rows(where, a, b, width, j), even, odd)

    def scaled(kind, j, mine_sum, other_sum):
        return amplitude(
            where, energies[kind], eps_rows, eps_cols, mine_sum, other_sum, j * width, half
        )

    jobs = [("local", 0), ("cross", 0), ("cross", 1), ("cross", 2), ("local", 1), ("local", 2)]
    n = len(jobs)
    left = {kind: sum(job[0] == kind for job in jobs) for kind in ("cross", "local")}
    own = {"cross": [], "local": []}
    part, inward, summed, across, amp, outward = ({} for _ in range(6))

    def settle(*values):
        order.last = (order.last, *values)

    hops = slabs // 2 - 1
    middle = [(hops, hops + 1), (hops + 1, hops)]

    def towards_middle(hop):
        return [(hop, hop + 1), (slabs - 1 - hop, slabs - 2 - hop)]

    def towards_ends(hop):
        return [(b, a) for a, b in towards_middle(hop)]

    def feed(s):
        value = product(*jobs[s])
        for hop in range(hops - 1):
            value = order.step(added, value, order.send(value, "aux", towards_middle(hop)))
        part[s] = value
        inward[s] = order.send(value, "aux", towards_middle(hops - 1))

    def pass_across(s):
        if 0 <= s < n:
            summed[s] = order.step(added, part[s], inward[s])
            across[s] = order.send(summed[s], "aux", middle)

    def pass_out(s):
        if 0 <= s < n:
            value = order.step(lambda a, b: scaled(*jobs[s], a, b), summed[s], across[s])
            for hop in reversed(range(1, hops)):
                value = order.step(
                    lambda a, b: picked(where, a, b, hop, slabs, 0, width, ()),
                    value, order.send(value, "aux", towards_ends(hop)),
                )
            amp[s] = value
            outward[s] = order.send(value, "aux", towards_ends(0))

    def collect(s):
        if 0 <= s < n:
            kind, j = jobs[s]
            together = kind == "cross"
            start, rows = (j * width, half) if together else (0, width)
            before = own[kind] if together else []
            full = order.step(
                lambda a, b, *c: picked(where, a, b, 0, slabs, start, rows, c), amp[s], outward[s], *before
            )
            own[kind] = [full] if together else own[kind] + [full]
            left[kind] -= 1

    def swapped(value):
        return order.send(value, "occ", swap_pairs)

    third = nvirt // 3
    spans = [(0, 2 * third), (2 * third, third)]
    kept, arrived = [], []

    def cross_term():
        j = len(kept)
        if j < len(spans) and cross_mix:
            kept.append(
                order.step(
                    lambda w, p, a, b: cross_columns(where, a, b, p, w, *spans[j]),
                    cross_mix[0], partner, received, upper,
                )
            )
            arrived.append(order.send(kept[j], "occ", back_pairs))

    cross_mix, other = [], []
    for s in range(-1, n + 2):
        if s + 1 < n:
            feed(s + 1)
        pass_across(s)
        if not cross_mix:
            pass_out(s - 1)
            collect(s - 2)
        else:
            collect(s - 2)
            pass_out(s - 1)
        if not left["cross"] and not cross_mix:
            cross_other = swapped(own["cross"][0])
            received = order.step(lambda *v: jnp.concatenate(v, axis=1), *incoming.values())
            upper = order.send(received, "occ", down_pairs)
            cross_mix = order.step(
                lambda a, b: mix(where, (a,), (b,), 0, slabs, count), own["cross"][0], cross_other
            )
            cross_term()
        elif s >= n:
            other += [swapped(v) for v in own["local"][len(other):]]
    while len(kept) < len(spans):
        cross_term()

    weight, dens = order.step(
        lambda *v: mix(where, v[:PIECES], v[PIECES:], 1, slabs, count), *own["local"], *other
    )
    total = order.step(lambda a, b: (a + b) * nvirt ** (-0.5), cross_mix[1], dens)
    density = total[0]
    moved = []
    for ahead in range(1, chips):
        pairs = [(i, (i + 2 * ahead) % count) for i in range(count)]
        moved.append(order.send(total[ahead].astype(BF16), "occ", pairs))
    gamma = order.step(
        lambda p, w, k, a: final_columns(where, p, w, k, a, *spans[0]), partner, weight, kept[0], arrived[0]
    )
    rest = order.step(lambda p, w: local_columns(p, w, *spans[1]), partner, weight)
    gamma = order.step(
        lambda r, k, a, g: closing_columns(where, r, k, a, *spans[1], g), rest, kept[1], arrived[1], gamma
    )
    density = order.step(lambda d, *m: d + sum(v.astype(F32) for v in m), density, *moved)
    return gamma, density


def solution(mesh):
    return jax.shard_map(
        shards,
        mesh=mesh,
        in_specs=(P(("grp", "occ"), "aux", None), P("grp"), P("grp"), P("grp")),
        out_specs=(P(("grp", "occ"), "aux", None), P(("grp", "aux"), "occ")),
        check_vma=False,
    )
```

```python
import functools

import jax
import jax.numpy as jnp
from jax import lax
from jax.experimental import pallas as pl
from jax.experimental.pallas import tpu as pltpu
from jax.sharding import PartitionSpec as P

F32 = jnp.float32
BF16 = jnp.bfloat16
PIECES = 3
LIMIT = 24 * 1024 * 1024
LIGHT = pl.CostEstimate(flops=10**9, bytes_accessed=10**6, transcendentals=0)

TINY = pl.CostEstimate(flops=10**7, bytes_accessed=10**4, transcendentals=0)


def contract(left, right, dim_left, dim_right):
    return lax.dot_general(
        left, right, (((dim_left,), (dim_right,)), ((), ())), preferred_element_type=F32
    )


class Order:
    def __init__(self, first):
        self.last = first

    def ready(self, *values):
        return lax.optimization_barrier((*values, self.last))[:-1]

    def step(self, work, *values):
        result = work(*self.ready(*values))
        self.last = result
        return result

    def send(self, value, axis, pairs, *others):
        return lax.ppermute(self.ready(value, *others)[0], axis, pairs)


def product_kernel(place, left, right, out):
    out[...] = contract(left[...], right[...], 0, 0).astype(BF16)


def product_rows(place, left, right, width, j):
    rows, nvirt = right.shape
    whole_left = left.shape[1] == width
    step = nvirt // 3
    return pl.pallas_call(
        product_kernel,
        grid_spec=pltpu.PrefetchScalarGridSpec(
            num_scalar_prefetch=1,
            grid=(nvirt // step,),
            in_specs=[
                pl.BlockSpec(
                    (rows, width), lambda i, p: (0, 0 if whole_left else p[0] * PIECES + j)
                ),
                pl.BlockSpec((rows, step), lambda i, p: (0, i)),
            ],
            out_specs=pl.BlockSpec((width, step), lambda i, p: (0, i)),
        ),
        out_shape=jax.ShapeDtypeStruct((width, nvirt), BF16),
        compiler_params=pltpu.CompilerParams(vmem_limit_bytes=LIMIT),
        cost_estimate=pl.CostEstimate(flops=300000000, bytes_accessed=10**4, transcendentals=0),
        name="slab_product",
    )(place, left, right)


def add_kernel(left, right, out):
    out[...] = (left[...].astype(F32) + right[...].astype(F32)).astype(BF16)


def added(left, right):
    return pl.pallas_call(
        add_kernel,
        out_shape=jax.ShapeDtypeStruct(left.shape, BF16),
        compiler_params=pltpu.CompilerParams(vmem_limit_bytes=LIMIT),
        cost_estimate=pl.CostEstimate(flops=2000000000, bytes_accessed=10**4, transcendentals=0),
        name="half_sum",
    )(left, right)


def pick_kernel(hop, slabs, place, left, right, *refs):
    out = refs[-1]
    outer = (place[1] == hop) | (place[1] == slabs - 1 - hop)

    @pl.when(outer)
    def _():
        out[...] = right[...]

    @pl.when(jnp.logical_not(outer))
    def _():
        out[...] = left[...]


def picked(place, left, right, hop, slabs, start, rows, before):
    width, nvirt = left.shape
    return pl.pallas_call(
        functools.partial(pick_kernel, hop, slabs),
        grid=(1,),
        in_specs=[pl.BlockSpec(memory_space=pltpu.SMEM)]
        + [pl.BlockSpec((width, nvirt), lambda i: (0, 0))] * 2
        + [pl.BlockSpec(memory_space=pl.ANY)] * len(before),
        out_specs=pl.BlockSpec((width, nvirt), lambda i: (start // width, 0)),
        out_shape=jax.ShapeDtypeStruct((rows, nvirt), BF16),
        input_output_aliases={3: 0} if before else {},
        compiler_params=pltpu.CompilerParams(vmem_limit_bytes=LIMIT),
        cost_estimate=pl.CostEstimate(flops=10000000, bytes_accessed=10**4, transcendentals=0),
        name="amp_of_slab",
    )(place, left, right, *before)


def amp_kernel(place, energy, eps_rows, eps_cols, left, right, out):
    denom = eps_rows[...] + eps_cols[...] - energy[0] - energy[1]
    out[...] = ((left[...].astype(F32) + right[...].astype(F32)) / denom).astype(BF16)


def amplitude(place, energy, eps_rows, eps_cols, left, right, start, half):
    width, nvirt = left.shape
    return pl.pallas_call(
        amp_kernel,
        grid_spec=pltpu.PrefetchScalarGridSpec(
            num_scalar_prefetch=1,
            grid=(1,),
            in_specs=[
                pl.BlockSpec(memory_space=pltpu.SMEM),
                pl.BlockSpec((width, 1), lambda i, p: (p[0] * (half // width) + start // width, 0)),
                pl.BlockSpec((1, nvirt), lambda i, p: (0, 0)),
                pl.BlockSpec((width, nvirt), lambda i, p: (0, 0)),
                pl.BlockSpec((width, nvirt), lambda i, p: (0, 0)),
            ],
            out_specs=pl.BlockSpec((width, nvirt), lambda i, p: (0, 0)),
        ),
        out_shape=jax.ShapeDtypeStruct(left.shape, BF16),
        compiler_params=pltpu.CompilerParams(vmem_limit_bytes=LIMIT),
        cost_estimate=pl.CostEstimate(flops=1000000000, bytes_accessed=10**4, transcendentals=0),
        name="amplitude",
    )(place, energy, eps_rows, eps_cols, left, right)


def mix_kernel(owned, half, band, rows, cols, straight_core, place, *refs):
    *pieces, mix, dens, amp_t, amp, sems = refs
    own, other = pieces[:owned], pieces[owned:]
    core, slab, chip = place[0], place[1], place[2]
    nvirt = 2 * half
    step = pl.program_id(0)

    @pl.when(step == 0)
    def _():
        copies = []
        for side, group in ((core, own), (1 - core, other)):
            start = side * half
            for piece in group:
                rows_at = pl.ds(pl.multiple_of(start, 128), piece.shape[0])
                copies.append(pltpu.make_async_copy(piece, amp_t.at[rows_at, :], sems.at[len(copies)]))
                start += piece.shape[0]
        for copy in copies:
            copy.start()
        for copy in copies:
            copy.wait()

    straight = core == straight_core
    here = jnp.where(straight, 2.0, -1.0).astype(F32)
    there = jnp.where(straight, -1.0, 2.0).astype(F32)
    start = pl.multiple_of(step * band, band)
    for j in range(nvirt // band):
        tile = amp_t[pl.ds(start, band), j * band : (j + 1) * band].astype(F32)
        turned = amp_t[j * band : (j + 1) * band, pl.ds(start, band)].astype(F32).T
        amp[pl.ds(start, band), j * band : (j + 1) * band] = turned.astype(BF16)
        mix[:, j * band : (j + 1) * band] = (here * tile + there * turned).astype(BF16)

    @pl.when(step == nvirt // band - 1)
    def _():
        chips = dens.shape[0]
        left = amp[pl.ds(pl.multiple_of(slab * rows, rows), rows), :]
        for ahead in range(chips):
            at = pl.multiple_of((2 * lax.rem(chip + ahead, chips) + core) * cols, cols)
            tilde = 2.0 * amp[pl.ds(at, cols), :].astype(F32) - amp_t[pl.ds(at, cols), :].astype(F32)
            dens[ahead] = contract(left, tilde.astype(BF16), 1, 1)


def mix(place, own, other, straight_core, slabs, count):
    nvirt = own[0].shape[1]
    rows, cols, chips = nvirt // slabs, nvirt // count, count // 2
    band = 256
    return pl.pallas_call(
        functools.partial(mix_kernel, len(own), nvirt // 2, band, rows, cols, straight_core),
        grid_spec=pltpu.PrefetchScalarGridSpec(
            num_scalar_prefetch=1,
            grid=(nvirt // band,),
            in_specs=[pl.BlockSpec(memory_space=pl.ANY)] * (len(own) + len(other)),
            out_specs=[
                pl.BlockSpec((band, nvirt), lambda i, p: (i, 0)),
                pl.BlockSpec((chips, rows, cols), lambda i, p: (0, 0, 0)),
            ],
            scratch_shapes=[
                pltpu.VMEM((nvirt, nvirt), BF16),
                pltpu.VMEM((nvirt, nvirt), BF16),
                pltpu.SemaphoreType.DMA((len(own) + len(other),)),
            ],
        ),
        out_shape=[
            jax.ShapeDtypeStruct((nvirt, nvirt), BF16),
            jax.ShapeDtypeStruct((chips, rows, cols), F32),
        ],
        compiler_params=pltpu.CompilerParams(vmem_limit_bytes=LIMIT),
        cost_estimate=pl.CostEstimate(flops=10000000, bytes_accessed=10**4, transcendentals=0),
        name="mix",
    )(place, *own, *other)


def block_of(rows):
    return 768 if rows % 768 == 0 else 128


def cross_kernel(place, lower, upper, partner, weight, out):
    half = lower.shape[1]

    @pl.when(place[0] == 0)
    def _():
        total = contract(lower[...], weight[:half, :], 1, 0)
        out[...] = (total + contract(upper[...], weight[half:, :], 1, 0)).astype(BF16)

    @pl.when(place[0] != 0)
    def _():
        out[...] = contract(partner[...], weight[...], 1, 0).astype(BF16)


def cross_columns(place, lower, upper, partner, weight, start, step):
    rows, nvirt = partner.shape
    block = block_of(rows)
    part = nvirt // 3
    return pl.pallas_call(
        cross_kernel,
        grid_spec=pltpu.PrefetchScalarGridSpec(
            num_scalar_prefetch=1,
            grid=(step // part, rows // block),
            in_specs=[
                pl.BlockSpec((block, nvirt // 2), lambda j, i, p: (jnp.where(p[0] == 0, i, 0), 0)),
                pl.BlockSpec((block, nvirt // 2), lambda j, i, p: (jnp.where(p[0] == 0, i, 0), 0)),
                pl.BlockSpec((block, nvirt), lambda j, i, p: (jnp.where(p[0] == 0, 0, i), 0)),
                pl.BlockSpec((nvirt, part), lambda j, i, p: (0, start // part + j)),
            ],
            out_specs=pl.BlockSpec((block, part), lambda j, i, p: (i, j)),
        ),
        out_shape=jax.ShapeDtypeStruct((rows, step), BF16),
        compiler_params=pltpu.CompilerParams(vmem_limit_bytes=LIMIT),
        cost_estimate=pl.CostEstimate(flops=4000000000, bytes_accessed=10**4, transcendentals=0),
        name="cross_term",
    )(place, lower, upper, partner, weight)


def final_kernel(place, partner, weight, kept, arrived, *refs):
    out = refs[-1]
    total = contract(partner[...], weight[...], 1, 0)

    @pl.when(place[0] == 0)
    def _():
        out[0] = (total.astype(BF16).astype(F32) + kept[...].astype(F32)).astype(BF16)

    @pl.when(place[0] != 0)
    def _():
        out[0] = (total + arrived[...].astype(F32)).astype(BF16)


def final_columns(place, partner, weight, kept, arrived, start, step, gamma=None):
    rows, nvirt = partner.shape
    block = block_of(rows)
    part = nvirt // 3
    before = [] if gamma is None else [gamma]
    return pl.pallas_call(
        final_kernel,
        grid_spec=pltpu.PrefetchScalarGridSpec(
            num_scalar_prefetch=1,
            grid=(step // part, rows // block),
            in_specs=[
                pl.BlockSpec((block, nvirt), lambda j, i, p: (i, 0)),
                pl.BlockSpec((nvirt, part), lambda j, i, p: (0, start // part + j)),
                pl.BlockSpec((block, part), lambda j, i, p: (jnp.where(p[0] == 0, i, 0), jnp.where(p[0] == 0, j, 0))),
                pl.BlockSpec((block, part), lambda j, i, p: (jnp.where(p[0] == 0, 0, i), jnp.where(p[0] == 0, 0, j))),
            ]
            + [pl.BlockSpec(memory_space=pl.ANY)] * len(before),
            out_specs=pl.BlockSpec((1, block, part), lambda j, i, p: (0, i, start // part + j)),
        ),
        out_shape=jax.ShapeDtypeStruct((1, rows, nvirt), BF16),
        input_output_aliases={5: 0} if before else {},
        compiler_params=pltpu.CompilerParams(vmem_limit_bytes=LIMIT),
        cost_estimate=pl.CostEstimate(flops=4000000000, bytes_accessed=10**4, transcendentals=0),
        name="local_term",
    )(place, partner, weight, kept, arrived, *before)


def local_kernel(partner, weight, out):
    out[...] = contract(partner[...], weight[...], 1, 0).astype(BF16)


def local_columns(partner, weight, start, step):
    rows, nvirt = partner.shape
    block = block_of(rows)
    part = nvirt // 3
    return pl.pallas_call(
        local_kernel,
        grid=(step // part, rows // block),
        in_specs=[
            pl.BlockSpec((block, nvirt), lambda j, i: (i, 0)),
            pl.BlockSpec((nvirt, part), lambda j, i: (0, start // part + j)),
        ],
        out_specs=pl.BlockSpec((block, part), lambda j, i: (i, j)),
        out_shape=jax.ShapeDtypeStruct((rows, step), BF16),
        compiler_params=pltpu.CompilerParams(vmem_limit_bytes=LIMIT),
        cost_estimate=pl.CostEstimate(flops=5760000000, bytes_accessed=10**4, transcendentals=0),
        name="local_rest",
    )(partner, weight)


def closing_kernel(place, rest, kept, arrived, gamma, out):
    @pl.when(place[0] == 0)
    def _():
        out[0] = (rest[...].astype(F32) + kept[...].astype(F32)).astype(BF16)

    @pl.when(place[0] != 0)
    def _():
        out[0] = (rest[...].astype(F32) + arrived[...].astype(F32)).astype(BF16)


def closing_columns(place, rest, kept, arrived, start, step, gamma):
    rows = rest.shape[0]
    part = 256
    return pl.pallas_call(
        closing_kernel,
        grid_spec=pltpu.PrefetchScalarGridSpec(
            num_scalar_prefetch=1,
            grid=(step // part,),
            in_specs=[
                pl.BlockSpec((rows, part), lambda i, p: (0, i)),
                pl.BlockSpec((rows, part), lambda i, p: (0, jnp.where(p[0] == 0, i, 0))),
                pl.BlockSpec((rows, part), lambda i, p: (0, jnp.where(p[0] == 0, 0, i))),
                pl.BlockSpec(memory_space=pl.ANY),
            ],
            out_specs=pl.BlockSpec((1, rows, part), lambda i, p: (0, 0, start // part + i)),
        ),
        out_shape=jax.ShapeDtypeStruct(gamma.shape, BF16),
        input_output_aliases={4: 0},
        compiler_params=pltpu.CompilerParams(vmem_limit_bytes=LIMIT),
        cost_estimate=TINY,
        name="closing_sum",
    )(place, rest, kept, arrived, gamma)


def shards(bmat, eps_occ, eps_vir, occ_label):
    count = lax.axis_size("occ")
    slabs = lax.axis_size("aux")
    place = lax.axis_index("occ")
    slab_index = lax.axis_index("aux")
    chips = count // 2
    chip, core = place // 2, place % 2
    first = core == 0
    where = jnp.stack([core, slab_index, chip]).astype(jnp.int32)
    nvirt = eps_vir.shape[0]
    half = nvirt // 2
    width = half // PIECES
    labels = jnp.arange(count, dtype=jnp.int32)
    energy = jnp.sum(
        eps_occ[None, :] * (occ_label[:, None] == labels[None, :]).astype(F32), axis=1
    )
    swap_pairs = [(i, i ^ 1) for i in range(count)]
    next_pairs = [(i, (i + 2) % count) for i in range(count)]
    down_pairs = [(i, i - 1) for i in range(1, count, 2)]
    back_pairs = [(i, (i - 2) % count) for i in range(1, count, 2)]

    def energy_at(row):
        return lax.dynamic_index_in_dim(energy, (row + count) % count, 0, keepdims=False)

    energies = {
        "cross": jnp.stack([energy_at(2 * chip), energy_at(2 * chip - 1)]),
        "local": jnp.stack([energy_at(2 * chip + 1), energy_at(2 * chip)]),
    }
    eps_rows, eps_cols = eps_vir.reshape(nvirt, 1), eps_vir.reshape(1, nvirt)

    mine = bmat[0]
    order = Order(where)
    incoming = {}

    def ship(j, low, high):
        sent = order.step(lambda a, b: jnp.where(first, a, b), low, high)
        incoming[j] = order.send(sent, "occ", next_pairs)

    def columns(value, start):
        return lax.slice_in_dim(value, start, start + width, axis=1)

    ship(0, order.send(columns(mine, 0), "occ", down_pairs), columns(mine, half))
    partner = order.send(mine, "occ", swap_pairs)
    ship(1, columns(partner, width), columns(mine, half + width))
    odd = order.step(lambda m, p: jnp.where(first, p, m), mine, partner)
    even = order.step(lambda m, p: jnp.where(first, m, p), mine, partner)

    def product(kind, j):
        if kind == "cross":
            part = order.step(lambda a, b: product_rows(where, a, b, width, j), incoming[j], even)
            if j + 2 < PIECES:
                ship(j + 2, columns(partner, (j + 2) * width), columns(mine, half + (j + 2) * width))
            return part
        return order.step(lambda a, b: product_rows(where, a, b, width, j), even, odd)

    def scaled(kind, j, mine_sum, other_sum):
        return amplitude(
            where, energies[kind], eps_rows, eps_cols, mine_sum, other_sum, j * width, half
        )

    jobs = [("local", 0), ("cross", 0), ("cross", 1), ("cross", 2), ("local", 1), ("local", 2)]
    n = len(jobs)
    left = {kind: sum(job[0] == kind for job in jobs) for kind in ("cross", "local")}
    own = {"cross": [], "local": []}
    part, inward, summed, across, amp, outward = ({} for _ in range(6))

    def settle(*values):
        order.last = (order.last, *values)

    hops = slabs // 2 - 1
    middle = [(hops, hops + 1), (hops + 1, hops)]

    def towards_middle(hop):
        return [(hop, hop + 1), (slabs - 1 - hop, slabs - 2 - hop)]

    def towards_ends(hop):
        return [(b, a) for a, b in towards_middle(hop)]

    def feed(s):
        value = product(*jobs[s])
        for hop in range(hops - 1):
            value = order.step(added, value, order.send(value, "aux", towards_middle(hop)))
        part[s] = value
        inward[s] = order.send(value, "aux", towards_middle(hops - 1))

    def pass_across(s):
        if 0 <= s < n:
            summed[s] = order.step(added, part[s], inward[s])
            across[s] = order.send(summed[s], "aux", middle)

    def pass_out(s):
        if 0 <= s < n:
            value = order.step(lambda a, b: scaled(*jobs[s], a, b), summed[s], across[s])
            for hop in reversed(range(1, hops)):
                value = order.step(
                    lambda a, b: picked(where, a, b, hop, slabs, 0, width, ()),
                    value, order.send(value, "aux", towards_ends(hop)),
                )
            amp[s] = value
            outward[s] = order.send(value, "aux", towards_ends(0))

    def collect(s):
        if 0 <= s < n:
            kind, j = jobs[s]
            together = kind == "cross"
            start, rows = (j * width, half) if together else (0, width)
            before = own[kind] if together else []
            full = order.step(
                lambda a, b, *c: picked(where, a, b, 0, slabs, start, rows, c), amp[s], outward[s], *before
            )
            own[kind] = [full] if together else own[kind] + [full]
            left[kind] -= 1

    def swapped(value):
        return order.send(value, "occ", swap_pairs)

    third = nvirt // 3
    spans = [(0, 2 * third), (2 * third, third)]
    kept, arrived = [], []

    def cross_term():
        j = len(kept)
        if j < len(spans) and cross_mix:
            kept.append(
                order.step(
                    lambda w, p, a, b: cross_columns(where, a, b, p, w, *spans[j]),
                    cross_mix[0], partner, received, upper,
                )
            )
            if j == 0:
                arrived.append(order.send(kept[j], "occ", back_pairs))

    cross_mix, other = [], []
    for s in range(-1, n + 2):
        if s + 1 < n:
            feed(s + 1)
        pass_across(s)
        if not cross_mix:
            pass_out(s - 1)
            collect(s - 2)
        else:
            if s == n + 1:
                cross_term()
            collect(s - 2)
            pass_out(s - 1)
        if not left["cross"] and not cross_mix:
            cross_other = swapped(own["cross"][0])
            received = order.step(lambda *v: jnp.concatenate(v, axis=1), *incoming.values())
            upper = order.send(received, "occ", down_pairs)
            cross_mix = order.step(
                lambda a, b: mix(where, (a,), (b,), 0, slabs, count), own["cross"][0], cross_other
            )
            cross_term()
        elif s >= n:
            other += [swapped(v) for v in own["local"][len(other):]]
    arrived.append(order.send(kept[1], "occ", back_pairs))

    weight, dens = order.step(
        lambda *v: mix(where, v[:PIECES], v[PIECES:], 1, slabs, count), *own["local"], *other
    )
    total = order.step(lambda a, b: (a + b) * nvirt ** (-0.5), cross_mix[1], dens)
    density = total[0]
    moved = []
    for ahead in range(1, chips):
        pairs = [(i, (i + 2 * ahead) % count) for i in range(count)]
        moved.append(order.send(total[ahead].astype(BF16), "occ", pairs))
    gamma = order.step(
        lambda p, w, k, a: final_columns(where, p, w, k, a, *spans[0]), partner, weight, kept[0], arrived[0]
    )
    rest = order.step(lambda p, w: local_columns(p, w, *spans[1]), partner, weight)
    gamma = order.step(
        lambda r, k, a, g: closing_columns(where, r, k, a, *spans[1], g), rest, kept[1], arrived[1], gamma
    )
    density = order.step(lambda d, *m: d + sum(v.astype(F32) for v in m), density, *moved)
    return gamma, density


def solution(mesh):
    return jax.shard_map(
        shards,
        mesh=mesh,
        in_specs=(P(("grp", "occ"), "aux", None), P("grp"), P("grp"), P("grp")),
        out_specs=(P(("grp", "occ"), "aux", None), P(("grp", "aux"), "occ")),
        check_vma=False,
    )
```

```python
import functools

import jax
import jax.numpy as jnp
from jax import lax
from jax.experimental import pallas as pl
from jax.experimental.pallas import tpu as pltpu
from jax.sharding import PartitionSpec as P

F32 = jnp.float32
BF16 = jnp.bfloat16
PIECES = 3
LIMIT = 24 * 1024 * 1024
LIGHT = pl.CostEstimate(flops=10**9, bytes_accessed=10**6, transcendentals=0)

TINY = pl.CostEstimate(flops=10**7, bytes_accessed=10**4, transcendentals=0)


def contract(left, right, dim_left, dim_right):
    return lax.dot_general(
        left, right, (((dim_left,), (dim_right,)), ((), ())), preferred_element_type=F32
    )


class Order:
    def __init__(self, first):
        self.last = first

    def ready(self, *values):
        return lax.optimization_barrier((*values, self.last))[:-1]

    def step(self, work, *values):
        result = work(*self.ready(*values))
        self.last = result
        return result

    def send(self, value, axis, pairs, *others):
        return lax.ppermute(self.ready(value, *others)[0], axis, pairs)


def product_kernel(place, left, right, out):
    out[...] = contract(left[...], right[...], 0, 0).astype(BF16)


def product_rows(place, left, right, width, j):
    rows, nvirt = right.shape
    whole_left = left.shape[1] == width
    step = nvirt // 3
    return pl.pallas_call(
        product_kernel,
        grid_spec=pltpu.PrefetchScalarGridSpec(
            num_scalar_prefetch=1,
            grid=(nvirt // step,),
            in_specs=[
                pl.BlockSpec(
                    (rows, width), lambda i, p: (0, 0 if whole_left else p[0] * PIECES + j)
                ),
                pl.BlockSpec((rows, step), lambda i, p: (0, i)),
            ],
            out_specs=pl.BlockSpec((width, step), lambda i, p: (0, i)),
        ),
        out_shape=jax.ShapeDtypeStruct((width, nvirt), BF16),
        compiler_params=pltpu.CompilerParams(vmem_limit_bytes=LIMIT),
        cost_estimate=pl.CostEstimate(flops=300000000, bytes_accessed=10**4, transcendentals=0),
        name="slab_product",
    )(place, left, right)


def add_kernel(left, right, out):
    out[...] = (left[...].astype(F32) + right[...].astype(F32)).astype(BF16)


def added(left, right):
    return pl.pallas_call(
        add_kernel,
        out_shape=jax.ShapeDtypeStruct(left.shape, BF16),
        compiler_params=pltpu.CompilerParams(vmem_limit_bytes=LIMIT),
        cost_estimate=pl.CostEstimate(flops=2000000000, bytes_accessed=10**4, transcendentals=0),
        name="half_sum",
    )(left, right)


def pick_kernel(hop, slabs, place, left, right, *refs):
    out = refs[-1]
    outer = (place[1] == hop) | (place[1] == slabs - 1 - hop)

    @pl.when(outer)
    def _():
        out[...] = right[...]

    @pl.when(jnp.logical_not(outer))
    def _():
        out[...] = left[...]


def picked(place, left, right, hop, slabs, start, rows, before):
    width, nvirt = left.shape
    return pl.pallas_call(
        functools.partial(pick_kernel, hop, slabs),
        grid=(1,),
        in_specs=[pl.BlockSpec(memory_space=pltpu.SMEM)]
        + [pl.BlockSpec((width, nvirt), lambda i: (0, 0))] * 2
        + [pl.BlockSpec(memory_space=pl.ANY)] * len(before),
        out_specs=pl.BlockSpec((width, nvirt), lambda i: (start // width, 0)),
        out_shape=jax.ShapeDtypeStruct((rows, nvirt), BF16),
        input_output_aliases={3: 0} if before else {},
        compiler_params=pltpu.CompilerParams(vmem_limit_bytes=LIMIT),
        cost_estimate=pl.CostEstimate(flops=10000000, bytes_accessed=10**4, transcendentals=0),
        name="amp_of_slab",
    )(place, left, right, *before)


def amp_kernel(place, energy, eps_rows, eps_cols, left, right, out):
    denom = eps_rows[...] + eps_cols[...] - energy[0] - energy[1]
    out[...] = ((left[...].astype(F32) + right[...].astype(F32)) / denom).astype(BF16)


def amplitude(place, energy, eps_rows, eps_cols, left, right, start, half):
    width, nvirt = left.shape
    return pl.pallas_call(
        amp_kernel,
        grid_spec=pltpu.PrefetchScalarGridSpec(
            num_scalar_prefetch=1,
            grid=(1,),
            in_specs=[
                pl.BlockSpec(memory_space=pltpu.SMEM),
                pl.BlockSpec((width, 1), lambda i, p: (p[0] * (half // width) + start // width, 0)),
                pl.BlockSpec((1, nvirt), lambda i, p: (0, 0)),
                pl.BlockSpec((width, nvirt), lambda i, p: (0, 0)),
                pl.BlockSpec((width, nvirt), lambda i, p: (0, 0)),
            ],
            out_specs=pl.BlockSpec((width, nvirt), lambda i, p: (0, 0)),
        ),
        out_shape=jax.ShapeDtypeStruct(left.shape, BF16),
        compiler_params=pltpu.CompilerParams(vmem_limit_bytes=LIMIT),
        cost_estimate=pl.CostEstimate(flops=1000000000, bytes_accessed=10**4, transcendentals=0),
        name="amplitude",
    )(place, energy, eps_rows, eps_cols, left, right)


def mix_kernel(owned, half, band, rows, cols, straight_core, place, *refs):
    *pieces, mix, dens, amp_t, amp, sems = refs
    own, other = pieces[:owned], pieces[owned:]
    core, slab, chip = place[0], place[1], place[2]
    nvirt = 2 * half
    step = pl.program_id(0)

    @pl.when(step == 0)
    def _():
        copies = []
        for side, group in ((core, own), (1 - core, other)):
            start = side * half
            for piece in group:
                rows_at = pl.ds(pl.multiple_of(start, 128), piece.shape[0])
                copies.append(pltpu.make_async_copy(piece, amp_t.at[rows_at, :], sems.at[len(copies)]))
                start += piece.shape[0]
        for copy in copies:
            copy.start()
        for copy in copies:
            copy.wait()

    straight = core == straight_core
    here = jnp.where(straight, 2.0, -1.0).astype(F32)
    there = jnp.where(straight, -1.0, 2.0).astype(F32)
    start = pl.multiple_of(step * band, band)
    for j in range(nvirt // band):
        tile = amp_t[pl.ds(start, band), j * band : (j + 1) * band].astype(F32)
        turned = amp_t[j * band : (j + 1) * band, pl.ds(start, band)].T
        amp[pl.ds(start, band), j * band : (j + 1) * band] = turned
        mix[:, j * band : (j + 1) * band] = (here * tile + there * turned.astype(F32)).astype(BF16)

    @pl.when(step == nvirt // band - 1)
    def _():
        chips = dens.shape[0]
        left = amp[pl.ds(pl.multiple_of(slab * rows, rows), rows), :]
        for ahead in range(chips):
            at = pl.multiple_of((2 * lax.rem(chip + ahead, chips) + core) * cols, cols)
            tilde = 2.0 * amp[pl.ds(at, cols), :].astype(F32) - amp_t[pl.ds(at, cols), :].astype(F32)
            dens[ahead] = contract(left, tilde.astype(BF16), 1, 1)


def mix(place, own, other, straight_core, slabs, count):
    nvirt = own[0].shape[1]
    rows, cols, chips = nvirt // slabs, nvirt // count, count // 2
    band = 256
    return pl.pallas_call(
        functools.partial(mix_kernel, len(own), nvirt // 2, band, rows, cols, straight_core),
        grid_spec=pltpu.PrefetchScalarGridSpec(
            num_scalar_prefetch=1,
            grid=(nvirt // band,),
            in_specs=[pl.BlockSpec(memory_space=pl.ANY)] * (len(own) + len(other)),
            out_specs=[
                pl.BlockSpec((band, nvirt), lambda i, p: (i, 0)),
                pl.BlockSpec((chips, rows, cols), lambda i, p: (0, 0, 0)),
            ],
            scratch_shapes=[
                pltpu.VMEM((nvirt, nvirt), BF16),
                pltpu.VMEM((nvirt, nvirt), BF16),
                pltpu.SemaphoreType.DMA((len(own) + len(other),)),
            ],
        ),
        out_shape=[
            jax.ShapeDtypeStruct((nvirt, nvirt), BF16),
            jax.ShapeDtypeStruct((chips, rows, cols), F32),
        ],
        compiler_params=pltpu.CompilerParams(vmem_limit_bytes=LIMIT),
        cost_estimate=pl.CostEstimate(flops=10000000, bytes_accessed=10**4, transcendentals=0),
        name="mix",
    )(place, *own, *other)


def block_of(rows):
    return 768 if rows % 768 == 0 else 128


def cross_kernel(place, lower, upper, partner, weight, out):
    half = lower.shape[1]

    @pl.when(place[0] == 0)
    def _():
        total = contract(lower[...], weight[:half, :], 1, 0)
        out[...] = (total + contract(upper[...], weight[half:, :], 1, 0)).astype(BF16)

    @pl.when(place[0] != 0)
    def _():
        out[...] = contract(partner[...], weight[...], 1, 0).astype(BF16)


def cross_columns(place, lower, upper, partner, weight, start, step):
    rows, nvirt = partner.shape
    block = block_of(rows)
    part = nvirt // 3
    return pl.pallas_call(
        cross_kernel,
        grid_spec=pltpu.PrefetchScalarGridSpec(
            num_scalar_prefetch=1,
            grid=(step // part, rows // block),
            in_specs=[
                pl.BlockSpec((block, nvirt // 2), lambda j, i, p: (jnp.where(p[0] == 0, i, 0), 0)),
                pl.BlockSpec((block, nvirt // 2), lambda j, i, p: (jnp.where(p[0] == 0, i, 0), 0)),
                pl.BlockSpec((block, nvirt), lambda j, i, p: (jnp.where(p[0] == 0, 0, i), 0)),
                pl.BlockSpec((nvirt, part), lambda j, i, p: (0, start // part + j)),
            ],
            out_specs=pl.BlockSpec((block, part), lambda j, i, p: (i, j)),
        ),
        out_shape=jax.ShapeDtypeStruct((rows, step), BF16),
        compiler_params=pltpu.CompilerParams(vmem_limit_bytes=LIMIT),
        cost_estimate=pl.CostEstimate(flops=4000000000, bytes_accessed=10**4, transcendentals=0),
        name="cross_term",
    )(place, lower, upper, partner, weight)


def final_kernel(place, partner, weight, kept, arrived, *refs):
    out = refs[-1]
    total = contract(partner[...], weight[...], 1, 0)

    @pl.when(place[0] == 0)
    def _():
        out[0] = (total.astype(BF16).astype(F32) + kept[...].astype(F32)).astype(BF16)

    @pl.when(place[0] != 0)
    def _():
        out[0] = (total + arrived[...].astype(F32)).astype(BF16)


def final_columns(place, partner, weight, kept, arrived, start, step, gamma=None):
    rows, nvirt = partner.shape
    block = block_of(rows)
    part = nvirt // 3
    before = [] if gamma is None else [gamma]
    return pl.pallas_call(
        final_kernel,
        grid_spec=pltpu.PrefetchScalarGridSpec(
            num_scalar_prefetch=1,
            grid=(step // part, rows // block),
            in_specs=[
                pl.BlockSpec((block, nvirt), lambda j, i, p: (i, 0)),
                pl.BlockSpec((nvirt, part), lambda j, i, p: (0, start // part + j)),
                pl.BlockSpec((block, part), lambda j, i, p: (jnp.where(p[0] == 0, i, 0), jnp.where(p[0] == 0, j, 0))),
                pl.BlockSpec((block, part), lambda j, i, p: (jnp.where(p[0] == 0, 0, i), jnp.where(p[0] == 0, 0, j))),
            ]
            + [pl.BlockSpec(memory_space=pl.ANY)] * len(before),
            out_specs=pl.BlockSpec((1, block, part), lambda j, i, p: (0, i, start // part + j)),
        ),
        out_shape=jax.ShapeDtypeStruct((1, rows, nvirt), BF16),
        input_output_aliases={5: 0} if before else {},
        compiler_params=pltpu.CompilerParams(vmem_limit_bytes=LIMIT),
        cost_estimate=pl.CostEstimate(flops=4000000000, bytes_accessed=10**4, transcendentals=0),
        name="local_term",
    )(place, partner, weight, kept, arrived, *before)


def local_kernel(partner, weight, out):
    out[...] = contract(partner[...], weight[...], 1, 0).astype(BF16)


def local_columns(partner, weight, start, step):
    rows, nvirt = partner.shape
    block = block_of(rows)
    part = nvirt // 3
    return pl.pallas_call(
        local_kernel,
        grid=(step // part, rows // block),
        in_specs=[
            pl.BlockSpec((block, nvirt), lambda j, i: (i, 0)),
            pl.BlockSpec((nvirt, part), lambda j, i: (0, start // part + j)),
        ],
        out_specs=pl.BlockSpec((block, part), lambda j, i: (i, j)),
        out_shape=jax.ShapeDtypeStruct((rows, step), BF16),
        compiler_params=pltpu.CompilerParams(vmem_limit_bytes=LIMIT),
        cost_estimate=pl.CostEstimate(flops=5760000000, bytes_accessed=10**4, transcendentals=0),
        name="local_rest",
    )(partner, weight)


def closing_kernel(place, rest, kept, arrived, gamma, out):
    @pl.when(place[0] == 0)
    def _():
        out[0] = (rest[...].astype(F32) + kept[...].astype(F32)).astype(BF16)

    @pl.when(place[0] != 0)
    def _():
        out[0] = (rest[...].astype(F32) + arrived[...].astype(F32)).astype(BF16)


def closing_columns(place, rest, kept, arrived, start, step, gamma):
    rows = rest.shape[0]
    part = 256
    return pl.pallas_call(
        closing_kernel,
        grid_spec=pltpu.PrefetchScalarGridSpec(
            num_scalar_prefetch=1,
            grid=(step // part,),
            in_specs=[
                pl.BlockSpec((rows, part), lambda i, p: (0, i)),
                pl.BlockSpec((rows, part), lambda i, p: (0, jnp.where(p[0] == 0, i, 0))),
                pl.BlockSpec((rows, part), lambda i, p: (0, jnp.where(p[0] == 0, 0, i))),
                pl.BlockSpec(memory_space=pl.ANY),
            ],
            out_specs=pl.BlockSpec((1, rows, part), lambda i, p: (0, 0, start // part + i)),
        ),
        out_shape=jax.ShapeDtypeStruct(gamma.shape, BF16),
        input_output_aliases={4: 0},
        compiler_params=pltpu.CompilerParams(vmem_limit_bytes=LIMIT),
        cost_estimate=TINY,
        name="closing_sum",
    )(place, rest, kept, arrived, gamma)


def shards(bmat, eps_occ, eps_vir, occ_label):
    count = lax.axis_size("occ")
    slabs = lax.axis_size("aux")
    place = lax.axis_index("occ")
    slab_index = lax.axis_index("aux")
    chips = count // 2
    chip, core = place // 2, place % 2
    first = core == 0
    where = jnp.stack([core, slab_index, chip]).astype(jnp.int32)
    nvirt = eps_vir.shape[0]
    half = nvirt // 2
    width = half // PIECES
    labels = jnp.arange(count, dtype=jnp.int32)
    energy = jnp.sum(
        eps_occ[None, :] * (occ_label[:, None] == labels[None, :]).astype(F32), axis=1
    )
    swap_pairs = [(i, i ^ 1) for i in range(count)]
    next_pairs = [(i, (i + 2) % count) for i in range(count)]
    down_pairs = [(i, i - 1) for i in range(1, count, 2)]
    back_pairs = [(i, (i - 2) % count) for i in range(1, count, 2)]

    def energy_at(row):
        return lax.dynamic_index_in_dim(energy, (row + count) % count, 0, keepdims=False)

    energies = {
        "cross": jnp.stack([energy_at(2 * chip), energy_at(2 * chip - 1)]),
        "local": jnp.stack([energy_at(2 * chip + 1), energy_at(2 * chip)]),
    }
    eps_rows, eps_cols = eps_vir.reshape(nvirt, 1), eps_vir.reshape(1, nvirt)

    mine = bmat[0]
    order = Order(where)
    incoming = {}

    def ship(j, low, high):
        sent = order.step(lambda a, b: jnp.where(first, a, b), low, high)
        incoming[j] = order.send(sent, "occ", next_pairs)

    def columns(value, start):
        return lax.slice_in_dim(value, start, start + width, axis=1)

    ship(0, order.send(columns(mine, 0), "occ", down_pairs), columns(mine, half))
    partner = order.send(mine, "occ", swap_pairs)
    ship(1, columns(partner, width), columns(mine, half + width))
    odd = order.step(lambda m, p: jnp.where(first, p, m), mine, partner)
    even = order.step(lambda m, p: jnp.where(first, m, p), mine, partner)

    def product(kind, j):
        if kind == "cross":
            part = order.step(lambda a, b: product_rows(where, a, b, width, j), incoming[j], even)
            if j + 2 < PIECES:
                ship(j + 2, columns(partner, (j + 2) * width), columns(mine, half + (j + 2) * width))
            return part
        return order.step(lambda a, b: product_rows(where, a, b, width, j), even, odd)

    def scaled(kind, j, mine_sum, other_sum):
        return amplitude(
            where, energies[kind], eps_rows, eps_cols, mine_sum, other_sum, j * width, half
        )

    jobs = [("local", 0), ("cross", 0), ("cross", 1), ("cross", 2), ("local", 1), ("local", 2)]
    n = len(jobs)
    left = {kind: sum(job[0] == kind for job in jobs) for kind in ("cross", "local")}
    own = {"cross": [], "local": []}
    part, inward, summed, across, amp, outward = ({} for _ in range(6))

    def settle(*values):
        order.last = (order.last, *values)

    hops = slabs // 2 - 1
    middle = [(hops, hops + 1), (hops + 1, hops)]

    def towards_middle(hop):
        return [(hop, hop + 1), (slabs - 1 - hop, slabs - 2 - hop)]

    def towards_ends(hop):
        return [(b, a) for a, b in towards_middle(hop)]

    def feed(s):
        value = product(*jobs[s])
        for hop in range(hops - 1):
            value = order.step(added, value, order.send(value, "aux", towards_middle(hop)))
        part[s] = value
        inward[s] = order.send(value, "aux", towards_middle(hops - 1))

    def pass_across(s):
        if 0 <= s < n:
            summed[s] = order.step(added, part[s], inward[s])
            across[s] = order.send(summed[s], "aux", middle)

    def pass_out(s):
        if 0 <= s < n:
            value = order.step(lambda a, b: scaled(*jobs[s], a, b), summed[s], across[s])
            for hop in reversed(range(1, hops)):
                value = order.step(
                    lambda a, b: picked(where, a, b, hop, slabs, 0, width, ()),
                    value, order.send(value, "aux", towards_ends(hop)),
                )
            amp[s] = value
            outward[s] = order.send(value, "aux", towards_ends(0))

    def collect(s):
        if 0 <= s < n:
            kind, j = jobs[s]
            together = kind == "cross"
            start, rows = (j * width, half) if together else (0, width)
            before = own[kind] if together else []
            full = order.step(
                lambda a, b, *c: picked(where, a, b, 0, slabs, start, rows, c), amp[s], outward[s], *before
            )
            own[kind] = [full] if together else own[kind] + [full]
            left[kind] -= 1

    def swapped(value):
        return order.send(value, "occ", swap_pairs)

    third = nvirt // 3
    spans = [(0, 2 * third), (2 * third, third)]
    kept, arrived = [], []

    def cross_term():
        j = len(kept)
        if j < len(spans) and cross_mix:
            kept.append(
                order.step(
                    lambda w, p, a, b: cross_columns(where, a, b, p, w, *spans[j]),
                    cross_mix[0], partner, received, upper,
                )
            )
            if j == 0:
                arrived.append(order.send(kept[j], "occ", back_pairs))

    cross_mix, other = [], []
    for s in range(-1, n + 2):
        if s + 1 < n:
            feed(s + 1)
        pass_across(s)
        if not cross_mix:
            pass_out(s - 1)
            collect(s - 2)
        else:
            if s == n + 1:
                cross_term()
            collect(s - 2)
            pass_out(s - 1)
        if not left["cross"] and not cross_mix:
            cross_other = swapped(own["cross"][0])
            received = order.step(lambda *v: jnp.concatenate(v, axis=1), *incoming.values())
            upper = order.send(received, "occ", down_pairs)
            cross_mix = order.step(
                lambda a, b: mix(where, (a,), (b,), 0, slabs, count), own["cross"][0], cross_other
            )
            cross_term()
        elif s >= n:
            other += [swapped(v) for v in own["local"][len(other):]]
    arrived.append(order.send(kept[1], "occ", back_pairs))

    weight, dens = order.step(
        lambda *v: mix(where, v[:PIECES], v[PIECES:], 1, slabs, count), *own["local"], *other
    )
    total = order.step(lambda a, b: (a + b) * nvirt ** (-0.5), cross_mix[1], dens)
    density = total[0]
    moved = []
    for ahead in range(1, chips):
        pairs = [(i, (i + 2 * ahead) % count) for i in range(count)]
        moved.append(order.send(total[ahead].astype(BF16), "occ", pairs))
    gamma = order.step(
        lambda p, w, k, a: final_columns(where, p, w, k, a, *spans[0]), partner, weight, kept[0], arrived[0]
    )
    rest = order.step(lambda p, w: local_columns(p, w, *spans[1]), partner, weight)
    gamma = order.step(
        lambda r, k, a, g: closing_columns(where, r, k, a, *spans[1], g), rest, kept[1], arrived[1], gamma
    )
    density = order.step(lambda d, *m: d + sum(v.astype(F32) for v in m), density, *moved)
    return gamma, density


def solution(mesh):
    return jax.shard_map(
        shards,
        mesh=mesh,
        in_specs=(P(("grp", "occ"), "aux", None), P("grp"), P("grp"), P("grp")),
        out_specs=(P(("grp", "occ"), "aux", None), P(("grp", "aux"), "occ")),
        check_vma=False,
    )
```

```python
import functools

import jax
import jax.numpy as jnp
from jax import lax
from jax.experimental import pallas as pl
from jax.experimental.pallas import tpu as pltpu
from jax.sharding import PartitionSpec as P

F32 = jnp.float32
BF16 = jnp.bfloat16
PIECES = 3
LIMIT = 24 * 1024 * 1024
LIGHT = pl.CostEstimate(flops=10**9, bytes_accessed=10**6, transcendentals=0)

TINY = pl.CostEstimate(flops=10**7, bytes_accessed=10**4, transcendentals=0)


def contract(left, right, dim_left, dim_right):
    return lax.dot_general(
        left, right, (((dim_left,), (dim_right,)), ((), ())), preferred_element_type=F32
    )


class Order:
    def __init__(self, first):
        self.last = first

    def ready(self, *values):
        return lax.optimization_barrier((*values, self.last))[:-1]

    def step(self, work, *values):
        result = work(*self.ready(*values))
        self.last = result
        return result

    def send(self, value, axis, pairs, *others):
        return lax.ppermute(self.ready(value, *others)[0], axis, pairs)


def product_kernel(place, left, right, out):
    out[...] = contract(left[...], right[...], 0, 0).astype(BF16)


def product_rows(place, left, right, width, j):
    rows, nvirt = right.shape
    whole_left = left.shape[1] == width
    step = nvirt // 3
    return pl.pallas_call(
        product_kernel,
        grid_spec=pltpu.PrefetchScalarGridSpec(
            num_scalar_prefetch=1,
            grid=(nvirt // step,),
            in_specs=[
                pl.BlockSpec(
                    (rows, width), lambda i, p: (0, 0 if whole_left else p[0] * PIECES + j)
                ),
                pl.BlockSpec((rows, step), lambda i, p: (0, i)),
            ],
            out_specs=pl.BlockSpec((width, step), lambda i, p: (0, i)),
        ),
        out_shape=jax.ShapeDtypeStruct((width, nvirt), BF16),
        compiler_params=pltpu.CompilerParams(vmem_limit_bytes=LIMIT),
        cost_estimate=pl.CostEstimate(flops=300000000, bytes_accessed=10**4, transcendentals=0),
        name="slab_product",
    )(place, left, right)


def add_kernel(left, right, out):
    out[...] = (left[...].astype(F32) + right[...].astype(F32)).astype(BF16)


def added(left, right):
    return pl.pallas_call(
        add_kernel,
        out_shape=jax.ShapeDtypeStruct(left.shape, BF16),
        compiler_params=pltpu.CompilerParams(vmem_limit_bytes=LIMIT),
        cost_estimate=pl.CostEstimate(flops=2000000000, bytes_accessed=10**4, transcendentals=0),
        name="half_sum",
    )(left, right)


def pick_kernel(hop, slabs, place, left, right, *refs):
    out = refs[-1]
    outer = (place[1] == hop) | (place[1] == slabs - 1 - hop)

    @pl.when(outer)
    def _():
        out[...] = right[...]

    @pl.when(jnp.logical_not(outer))
    def _():
        out[...] = left[...]


def picked(place, left, right, hop, slabs, start, rows, before):
    width, nvirt = left.shape
    return pl.pallas_call(
        functools.partial(pick_kernel, hop, slabs),
        grid=(1,),
        in_specs=[pl.BlockSpec(memory_space=pltpu.SMEM)]
        + [pl.BlockSpec((width, nvirt), lambda i: (0, 0))] * 2
        + [pl.BlockSpec(memory_space=pl.ANY)] * len(before),
        out_specs=pl.BlockSpec((width, nvirt), lambda i: (start // width, 0)),
        out_shape=jax.ShapeDtypeStruct((rows, nvirt), BF16),
        input_output_aliases={3: 0} if before else {},
        compiler_params=pltpu.CompilerParams(vmem_limit_bytes=LIMIT),
        cost_estimate=pl.CostEstimate(flops=10000000, bytes_accessed=10**4, transcendentals=0),
        name="amp_of_slab",
    )(place, left, right, *before)


def amp_kernel(place, energy, eps_rows, eps_cols, left, right, out):
    denom = eps_rows[...] + eps_cols[...] - energy[0] - energy[1]
    out[...] = ((left[...].astype(F32) + right[...].astype(F32)) / denom).astype(BF16)


def amplitude(place, energy, eps_rows, eps_cols, left, right, start, half):
    width, nvirt = left.shape
    return pl.pallas_call(
        amp_kernel,
        grid_spec=pltpu.PrefetchScalarGridSpec(
            num_scalar_prefetch=1,
            grid=(1,),
            in_specs=[
                pl.BlockSpec(memory_space=pltpu.SMEM),
                pl.BlockSpec((width, 1), lambda i, p: (p[0] * (half // width) + start // width, 0)),
                pl.BlockSpec((1, nvirt), lambda i, p: (0, 0)),
                pl.BlockSpec((width, nvirt), lambda i, p: (0, 0)),
                pl.BlockSpec((width, nvirt), lambda i, p: (0, 0)),
            ],
            out_specs=pl.BlockSpec((width, nvirt), lambda i, p: (0, 0)),
        ),
        out_shape=jax.ShapeDtypeStruct(left.shape, BF16),
        compiler_params=pltpu.CompilerParams(vmem_limit_bytes=LIMIT),
        cost_estimate=pl.CostEstimate(flops=1000000000, bytes_accessed=10**4, transcendentals=0),
        name="amplitude",
    )(place, energy, eps_rows, eps_cols, left, right)


def mix_kernel(owned, half, band, rows, cols, straight_core, place, *refs):
    *pieces, mix, dens, amp_t, amp, sems = refs
    own, other = pieces[:owned], pieces[owned:]
    core, slab, chip = place[0], place[1], place[2]
    nvirt = 2 * half
    step = pl.program_id(0)

    @pl.when(step == 0)
    def _():
        copies = []
        for side, group in ((core, own), (1 - core, other)):
            start = side * half
            for piece in group:
                rows_at = pl.ds(pl.multiple_of(start, 128), piece.shape[0])
                copies.append(pltpu.make_async_copy(piece, amp_t.at[rows_at, :], sems.at[len(copies)]))
                start += piece.shape[0]
        for copy in copies:
            copy.start()
        for copy in copies:
            copy.wait()

    straight = core == straight_core
    here = jnp.where(straight, 2.0, -1.0).astype(F32)
    there = jnp.where(straight, -1.0, 2.0).astype(F32)
    start = pl.multiple_of(step * band, band)
    for j in range(nvirt // band):
        tile = amp_t[pl.ds(start, band), j * band : (j + 1) * band].astype(F32)
        turned = amp_t[j * band : (j + 1) * band, pl.ds(start, band)].T
        amp[pl.ds(start, band), j * band : (j + 1) * band] = turned
        mix[:, j * band : (j + 1) * band] = (here * tile + there * turned.astype(F32)).astype(BF16)

    @pl.when(step == nvirt // band - 1)
    def _():
        chips = dens.shape[0]
        left = amp[pl.ds(pl.multiple_of(slab * rows, rows), rows), :]
        for ahead in range(chips):
            at = pl.multiple_of((2 * lax.rem(chip + ahead, chips) + core) * cols, cols)
            tilde = 2.0 * amp[pl.ds(at, cols), :].astype(F32) - amp_t[pl.ds(at, cols), :].astype(F32)
            dens[ahead] = contract(left, tilde.astype(BF16), 1, 1)


def mix(place, own, other, straight_core, slabs, count):
    nvirt = own[0].shape[1]
    rows, cols, chips = nvirt // slabs, nvirt // count, count // 2
    band = 512
    return pl.pallas_call(
        functools.partial(mix_kernel, len(own), nvirt // 2, band, rows, cols, straight_core),
        grid_spec=pltpu.PrefetchScalarGridSpec(
            num_scalar_prefetch=1,
            grid=(nvirt // band,),
            in_specs=[pl.BlockSpec(memory_space=pl.ANY)] * (len(own) + len(other)),
            out_specs=[
                pl.BlockSpec((band, nvirt), lambda i, p: (i, 0)),
                pl.BlockSpec((chips, rows, cols), lambda i, p: (0, 0, 0)),
            ],
            scratch_shapes=[
                pltpu.VMEM((nvirt, nvirt), BF16),
                pltpu.VMEM((nvirt, nvirt), BF16),
                pltpu.SemaphoreType.DMA((len(own) + len(other),)),
            ],
        ),
        out_shape=[
            jax.ShapeDtypeStruct((nvirt, nvirt), BF16),
            jax.ShapeDtypeStruct((chips, rows, cols), F32),
        ],
        compiler_params=pltpu.CompilerParams(vmem_limit_bytes=LIMIT),
        cost_estimate=pl.CostEstimate(flops=10000000, bytes_accessed=10**4, transcendentals=0),
        name="mix",
    )(place, *own, *other)


def block_of(rows):
    return 768 if rows % 768 == 0 else 128


def cross_kernel(place, lower, upper, partner, weight, out):
    half = lower.shape[1]

    @pl.when(place[0] == 0)
    def _():
        total = contract(lower[...], weight[:half, :], 1, 0)
        out[...] = (total + contract(upper[...], weight[half:, :], 1, 0)).astype(BF16)

    @pl.when(place[0] != 0)
    def _():
        out[...] = contract(partner[...], weight[...], 1, 0).astype(BF16)


def cross_columns(place, lower, upper, partner, weight, start, step):
    rows, nvirt = partner.shape
    block = block_of(rows)
    part = nvirt // 3
    return pl.pallas_call(
        cross_kernel,
        grid_spec=pltpu.PrefetchScalarGridSpec(
            num_scalar_prefetch=1,
            grid=(step // part, rows // block),
            in_specs=[
                pl.BlockSpec((block, nvirt // 2), lambda j, i, p: (jnp.where(p[0] == 0, i, 0), 0)),
                pl.BlockSpec((block, nvirt // 2), lambda j, i, p: (jnp.where(p[0] == 0, i, 0), 0)),
                pl.BlockSpec((block, nvirt), lambda j, i, p: (jnp.where(p[0] == 0, 0, i), 0)),
                pl.BlockSpec((nvirt, part), lambda j, i, p: (0, start // part + j)),
            ],
            out_specs=pl.BlockSpec((block, part), lambda j, i, p: (i, j)),
        ),
        out_shape=jax.ShapeDtypeStruct((rows, step), BF16),
        compiler_params=pltpu.CompilerParams(vmem_limit_bytes=LIMIT),
        cost_estimate=pl.CostEstimate(flops=4000000000, bytes_accessed=10**4, transcendentals=0),
        name="cross_term",
    )(place, lower, upper, partner, weight)


def final_kernel(place, partner, weight, kept, arrived, *refs):
    out = refs[-1]
    total = contract(partner[...], weight[...], 1, 0)

    @pl.when(place[0] == 0)
    def _():
        out[0] = (total.astype(BF16).astype(F32) + kept[...].astype(F32)).astype(BF16)

    @pl.when(place[0] != 0)
    def _():
        out[0] = (total + arrived[...].astype(F32)).astype(BF16)


def final_columns(place, partner, weight, kept, arrived, start, step, gamma=None):
    rows, nvirt = partner.shape
    block = block_of(rows)
    part = nvirt // 3
    before = [] if gamma is None else [gamma]
    return pl.pallas_call(
        final_kernel,
        grid_spec=pltpu.PrefetchScalarGridSpec(
            num_scalar_prefetch=1,
            grid=(step // part, rows // block),
            in_specs=[
                pl.BlockSpec((block, nvirt), lambda j, i, p: (i, 0)),
                pl.BlockSpec((nvirt, part), lambda j, i, p: (0, start // part + j)),
                pl.BlockSpec((block, part), lambda j, i, p: (jnp.where(p[0] == 0, i, 0), jnp.where(p[0] == 0, j, 0))),
                pl.BlockSpec((block, part), lambda j, i, p: (jnp.where(p[0] == 0, 0, i), jnp.where(p[0] == 0, 0, j))),
            ]
            + [pl.BlockSpec(memory_space=pl.ANY)] * len(before),
            out_specs=pl.BlockSpec((1, block, part), lambda j, i, p: (0, i, start // part + j)),
        ),
        out_shape=jax.ShapeDtypeStruct((1, rows, nvirt), BF16),
        input_output_aliases={5: 0} if before else {},
        compiler_params=pltpu.CompilerParams(vmem_limit_bytes=LIMIT),
        cost_estimate=pl.CostEstimate(flops=4000000000, bytes_accessed=10**4, transcendentals=0),
        name="local_term",
    )(place, partner, weight, kept, arrived, *before)


def local_kernel(partner, weight, out):
    out[...] = contract(partner[...], weight[...], 1, 0).astype(BF16)


def local_columns(partner, weight, start, step):
    rows, nvirt = partner.shape
    block = block_of(rows)
    part = nvirt // 3
    return pl.pallas_call(
        local_kernel,
        grid=(step // part, rows // block),
        in_specs=[
            pl.BlockSpec((block, nvirt), lambda j, i: (i, 0)),
            pl.BlockSpec((nvirt, part), lambda j, i: (0, start // part + j)),
        ],
        out_specs=pl.BlockSpec((block, part), lambda j, i: (i, j)),
        out_shape=jax.ShapeDtypeStruct((rows, step), BF16),
        compiler_params=pltpu.CompilerParams(vmem_limit_bytes=LIMIT),
        cost_estimate=pl.CostEstimate(flops=5760000000, bytes_accessed=10**4, transcendentals=0),
        name="local_rest",
    )(partner, weight)


def closing_kernel(place, rest, kept, arrived, gamma, out):
    @pl.when(place[0] == 0)
    def _():
        out[0] = (rest[...].astype(F32) + kept[...].astype(F32)).astype(BF16)

    @pl.when(place[0] != 0)
    def _():
        out[0] = (rest[...].astype(F32) + arrived[...].astype(F32)).astype(BF16)


def closing_columns(place, rest, kept, arrived, start, step, gamma):
    rows = rest.shape[0]
    part = 256
    return pl.pallas_call(
        closing_kernel,
        grid_spec=pltpu.PrefetchScalarGridSpec(
            num_scalar_prefetch=1,
            grid=(step // part,),
            in_specs=[
                pl.BlockSpec((rows, part), lambda i, p: (0, i)),
                pl.BlockSpec((rows, part), lambda i, p: (0, jnp.where(p[0] == 0, i, 0))),
                pl.BlockSpec((rows, part), lambda i, p: (0, jnp.where(p[0] == 0, 0, i))),
                pl.BlockSpec(memory_space=pl.ANY),
            ],
            out_specs=pl.BlockSpec((1, rows, part), lambda i, p: (0, 0, start // part + i)),
        ),
        out_shape=jax.ShapeDtypeStruct(gamma.shape, BF16),
        input_output_aliases={4: 0},
        compiler_params=pltpu.CompilerParams(vmem_limit_bytes=LIMIT),
        cost_estimate=TINY,
        name="closing_sum",
    )(place, rest, kept, arrived, gamma)


def shards(bmat, eps_occ, eps_vir, occ_label):
    count = lax.axis_size("occ")
    slabs = lax.axis_size("aux")
    place = lax.axis_index("occ")
    slab_index = lax.axis_index("aux")
    chips = count // 2
    chip, core = place // 2, place % 2
    first = core == 0
    where = jnp.stack([core, slab_index, chip]).astype(jnp.int32)
    nvirt = eps_vir.shape[0]
    half = nvirt // 2
    width = half // PIECES
    labels = jnp.arange(count, dtype=jnp.int32)
    energy = jnp.sum(
        eps_occ[None, :] * (occ_label[:, None] == labels[None, :]).astype(F32), axis=1
    )
    swap_pairs = [(i, i ^ 1) for i in range(count)]
    next_pairs = [(i, (i + 2) % count) for i in range(count)]
    down_pairs = [(i, i - 1) for i in range(1, count, 2)]
    back_pairs = [(i, (i - 2) % count) for i in range(1, count, 2)]

    def energy_at(row):
        return lax.dynamic_index_in_dim(energy, (row + count) % count, 0, keepdims=False)

    energies = {
        "cross": jnp.stack([energy_at(2 * chip), energy_at(2 * chip - 1)]),
        "local": jnp.stack([energy_at(2 * chip + 1), energy_at(2 * chip)]),
    }
    eps_rows, eps_cols = eps_vir.reshape(nvirt, 1), eps_vir.reshape(1, nvirt)

    mine = bmat[0]
    order = Order(where)
    incoming = {}

    def ship(j, low, high):
        sent = order.step(lambda a, b: jnp.where(first, a, b), low, high)
        incoming[j] = order.send(sent, "occ", next_pairs)

    def columns(value, start):
        return lax.slice_in_dim(value, start, start + width, axis=1)

    ship(0, order.send(columns(mine, 0), "occ", down_pairs), columns(mine, half))
    partner = order.send(mine, "occ", swap_pairs)
    ship(1, columns(partner, width), columns(mine, half + width))
    odd = order.step(lambda m, p: jnp.where(first, p, m), mine, partner)
    even = order.step(lambda m, p: jnp.where(first, m, p), mine, partner)

    def product(kind, j):
        if kind == "cross":
            part = order.step(lambda a, b: product_rows(where, a, b, width, j), incoming[j], even)
            if j + 2 < PIECES:
                ship(j + 2, columns(partner, (j + 2) * width), columns(mine, half + (j + 2) * width))
            return part
        return order.step(lambda a, b: product_rows(where, a, b, width, j), even, odd)

    def scaled(kind, j, mine_sum, other_sum):
        return amplitude(
            where, energies[kind], eps_rows, eps_cols, mine_sum, other_sum, j * width, half
        )

    jobs = [("local", 0), ("cross", 0), ("cross", 1), ("cross", 2), ("local", 1), ("local", 2)]
    n = len(jobs)
    left = {kind: sum(job[0] == kind for job in jobs) for kind in ("cross", "local")}
    own = {"cross": [], "local": []}
    part, inward, summed, across, amp, outward = ({} for _ in range(6))

    def settle(*values):
        order.last = (order.last, *values)

    hops = slabs // 2 - 1
    middle = [(hops, hops + 1), (hops + 1, hops)]

    def towards_middle(hop):
        return [(hop, hop + 1), (slabs - 1 - hop, slabs - 2 - hop)]

    def towards_ends(hop):
        return [(b, a) for a, b in towards_middle(hop)]

    def feed(s):
        value = product(*jobs[s])
        for hop in range(hops - 1):
            value = order.step(added, value, order.send(value, "aux", towards_middle(hop)))
        part[s] = value
        inward[s] = order.send(value, "aux", towards_middle(hops - 1))

    def pass_across(s):
        if 0 <= s < n:
            summed[s] = order.step(added, part[s], inward[s])
            across[s] = order.send(summed[s], "aux", middle)

    def pass_out(s):
        if 0 <= s < n:
            value = order.step(lambda a, b: scaled(*jobs[s], a, b), summed[s], across[s])
            for hop in reversed(range(1, hops)):
                value = order.step(
                    lambda a, b: picked(where, a, b, hop, slabs, 0, width, ()),
                    value, order.send(value, "aux", towards_ends(hop)),
                )
            amp[s] = value
            outward[s] = order.send(value, "aux", towards_ends(0))

    def collect(s):
        if 0 <= s < n:
            kind, j = jobs[s]
            together = kind == "cross"
            start, rows = (j * width, half) if together else (0, width)
            before = own[kind] if together else []
            full = order.step(
                lambda a, b, *c: picked(where, a, b, 0, slabs, start, rows, c), amp[s], outward[s], *before
            )
            own[kind] = [full] if together else own[kind] + [full]
            left[kind] -= 1

    def swapped(value):
        return order.send(value, "occ", swap_pairs)

    third = nvirt // 3
    spans = [(0, 2 * third), (2 * third, third)]
    kept, arrived = [], []

    def cross_term():
        j = len(kept)
        if j < len(spans) and cross_mix:
            kept.append(
                order.step(
                    lambda w, p, a, b: cross_columns(where, a, b, p, w, *spans[j]),
                    cross_mix[0], partner, received, upper,
                )
            )
            if j == 0:
                arrived.append(order.send(kept[j], "occ", back_pairs))

    cross_mix, other = [], []
    for s in range(-1, n + 2):
        if s + 1 < n:
            feed(s + 1)
        pass_across(s)
        if not cross_mix:
            pass_out(s - 1)
            collect(s - 2)
        else:
            if s == n + 1:
                cross_term()
            collect(s - 2)
            pass_out(s - 1)
        if not left["cross"] and not cross_mix:
            cross_other = swapped(own["cross"][0])
            received = order.step(lambda *v: jnp.concatenate(v, axis=1), *incoming.values())
            upper = order.send(received, "occ", down_pairs)
            cross_mix = order.step(
                lambda a, b: mix(where, (a,), (b,), 0, slabs, count), own["cross"][0], cross_other
            )
            cross_term()
        elif s >= n:
            other += [swapped(v) for v in own["local"][len(other):]]
    arrived.append(order.send(kept[1], "occ", back_pairs))

    weight, dens = order.step(
        lambda *v: mix(where, v[:PIECES], v[PIECES:], 1, slabs, count), *own["local"], *other
    )
    total = order.step(lambda a, b: (a + b) * nvirt ** (-0.5), cross_mix[1], dens)
    density = total[0]
    moved = []
    for ahead in range(1, chips):
        pairs = [(i, (i + 2 * ahead) % count) for i in range(count)]
        moved.append(order.send(total[ahead].astype(BF16), "occ", pairs))
    gamma = order.step(
        lambda p, w, k, a: final_columns(where, p, w, k, a, *spans[0]), partner, weight, kept[0], arrived[0]
    )
    rest = order.step(lambda p, w: local_columns(p, w, *spans[1]), partner, weight)
    gamma = order.step(
        lambda r, k, a, g: closing_columns(where, r, k, a, *spans[1], g), rest, kept[1], arrived[1], gamma
    )
    density = order.step(lambda d, *m: d + sum(v.astype(F32) for v in m), density, *moved)
    return gamma, density


def solution(mesh):
    return jax.shard_map(
        shards,
        mesh=mesh,
        in_specs=(P(("grp", "occ"), "aux", None), P("grp"), P("grp"), P("grp")),
        out_specs=(P(("grp", "occ"), "aux", None), P(("grp", "aux"), "occ")),
        check_vma=False,
    )
```
